128 devices in a mesh: leaf: 32 (over y, z, core), slab: 4 (over x).
Axes of the slice: x: 4, y: 4, z: 4, core: 2. Of those that a mesh axis runs over, the one named last changes fastest.
Arguments:
- sources: bfloat16 [8192, 16, 256], P(('slab', 'leaf')), may hold values from -6 to 6
- source_basis: bfloat16 [8192, 64, 256], P(('slab', 'leaf')), may hold values from -0.375 to 0.375
- target_basis: bfloat16 [8192, 64, 256], P(('slab', 'leaf')), may hold values from -0.75 to 0.75
- up_leaf: float32 [8192, 64, 64], P(('slab', 'leaf')), may hold values from -0.375 to 0.375
- down_leaf: float32 [8192, 64, 64], P(('slab', 'leaf')), may hold values from -0.75 to 0.75
- up_section: float32 [2048, 64, 64], P(('slab', 'leaf')), may hold values from -0.09375 to 0.09375
- down_section: float32 [2048, 64, 64], P(('slab', 'leaf')), may hold values from -0.75 to 0.75
- section_coupling: float32 [2048, 8, 64, 64], P(('slab', 'leaf')), may hold values from -0.25 to 0.25
- top_coupling: float32 [32, 8, 64, 64], P('slab'), may hold values from -0.25 to 0.25
- near_blocks: bfloat16 [9, 256, 256], replicated, may hold values from -0.125 to 0.125
- leaf_parent: int32 [8192], P(('slab', 'leaf')), may hold values from 0 to 2047, as said below
- near_list: int32 [8192, 9], P(('slab', 'leaf')), may hold values from 0 to 8191, as said below
- section_list: int32 [2048, 8], P(('slab', 'leaf')), may hold values from 0 to 2047, as said below
- top_list: int32 [32, 8], P('slab'), may hold values from 0 to 31, as said below
Outputs:
- potential: bfloat16 [8192, 16, 256], P(('slab', 'leaf'))
The draws below stay inside these ranges and needn't reach their ends.
Inputs may be any that keep to these rules, and one draw needn't show every extreme that they name: `leaf_parent`: the section box is held by the same device as the leaf box; each section box is named by exactly 4 leaf boxes. `near_list`: let leaf box b be held by device (s, i). Its 9 entries name boxes on the nine devices (s + a mod 4, i + c mod 32) for a, c in -1, 0, 1, one entry on each. `section_list`: each entry names a section box on the device one step lower or one step higher along leaf (cyclically) in the same slab; every section box has entries on both. `top_list`: no top box is coupled to itself.
All inputs are finite; a program needn't handle non-finite values.
Results may differ from the reference program's by a relative error of at most 0.0046.
Values may be sent and summed in bfloat16 or wider, within the bound.
No kernel may reach another device: no remote copies, remote signals or barrier semaphores. Data moves between devices by JAX's collectives and lax.ppermute only.
A program may use at most 128 MiB of HBM per device.

```python
import jax
import jax.numpy as jnp
from jax import lax

P_SIZE = 256
K = 64
R = 16
LB = 64
CH = 4
GROUP = 4
NEAR = 9
C1 = 8
C2 = 8
PB = 16
BOXES = 8192
SECTIONS = 2048
TOPS = 32
N_LEAF = 32
N_SLAB = 4


def draw_leaf_parent(key, part):
    key = jax.random.fold_in(key, 11)
    devices_all = N_SLAB * N_LEAF
    keys = jax.random.split(key, devices_all)
    orders = jax.vmap(lambda single: jax.random.permutation(single, LB))(keys)
    owners = jnp.arange(devices_all, dtype=jnp.int32)[:, None]
    return (owners * PB + orders.astype(jnp.int32) // CH).reshape(-1).astype(jnp.int32)


def draw_near_list(key, part):
    key = jax.random.fold_in(key, 12)
    first_key, second_key = jax.random.split(key)
    shifts = jax.random.randint(first_key, (BOXES,), 0, 9)
    within = jax.random.randint(second_key, (BOXES, NEAR), 0, LB)
    offsets = (shifts[:, None] + jnp.arange(NEAR, dtype=jnp.int32)[None, :]) % 9
    owner = jnp.arange(BOXES, dtype=jnp.int32) // LB
    slab_pos = (owner // N_LEAF)[:, None]
    leaf_pos = (owner % N_LEAF)[:, None]
    new_slab = (slab_pos + offsets // 3 - 1 + N_SLAB) % N_SLAB
    new_leaf = (leaf_pos + offsets % 3 - 1 + N_LEAF) % N_LEAF
    return ((new_slab * N_LEAF + new_leaf) * LB + within).astype(jnp.int32)


def draw_section_list(key, part):
    key = jax.random.fold_in(key, 13)
    first_key, second_key, third_key = jax.random.split(key, 3)
    sides = jax.random.randint(first_key, (SECTIONS, C1), 0, 2)
    lead = jax.random.randint(third_key, (SECTIONS,), 0, 2)
    column = jnp.arange(C1, dtype=jnp.int32)[None, :]
    sides = jnp.where(column == 0, lead[:, None], jnp.where(column == 1, 1 - lead[:, None], sides))
    within = jax.random.randint(second_key, (SECTIONS, C1), 0, PB)
    owner = jnp.arange(SECTIONS, dtype=jnp.int32) // PB
    slab_pos = (owner // N_LEAF)[:, None]
    leaf_pos = (owner % N_LEAF)[:, None]
    new_leaf = (leaf_pos + 2 * sides - 1 + N_LEAF) % N_LEAF
    return ((slab_pos * N_LEAF + new_leaf) * PB + within).astype(jnp.int32)


def draw_top_list(key, part):
    key = jax.random.fold_in(key, 14)
    steps = jax.random.randint(key, (TOPS, C2), 1, TOPS)
    return ((jnp.arange(TOPS, dtype=jnp.int32)[:, None] + steps) % TOPS).astype(jnp.int32)


def levels(stream_key, shape, shards, least, high):
    factor_of = 1.0
    for dim, parts in shards:
        heights = jax.random.uniform(jax.random.fold_in(jax.random.fold_in(stream_key, 6), dim), (parts,), jnp.float32, least / len(shards), high / len(shards))
        factor_of = factor_of * jnp.repeat(jnp.exp(heights), shape[dim] // parts).reshape((-1,) + (1,) * (len(shape) - 1 - dim))
    return factor_of


def noise(rng, shape, width, reach, shards=(), kind=jnp.bfloat16):
    array = jax.random.normal(rng, shape, jnp.float32) * width
    if len(shards) > 0:
        array = levels(rng, shape, shards, -0.22, 0.18) * array
    return jnp.clip(array, min=-reach, max=reach).astype(kind)


def setup_inputs(seed: int = 0) -> dict:
    streams_of = jax.random.split(jax.random.key(seed), 15)
    return {
        "sources": noise(streams_of[0], (BOXES, R, P_SIZE), 1.0, 6.0, ((0, 128),)),
        "source_basis": noise(streams_of[1], (BOXES, K, P_SIZE), P_SIZE ** -0.5, 0.375, ((0, 128),)),
        "target_basis": noise(streams_of[2], (BOXES, K, P_SIZE), K ** -0.5, 0.75, ((0, 128),)),
        "up_leaf": noise(streams_of[3], (BOXES, K, K), (CH * K) ** -0.5, 0.375, ((0, 128),), jnp.float32),
        "down_leaf": noise(streams_of[4], (BOXES, K, K), K ** -0.5, 0.75, ((0, 128),), jnp.float32),
        "up_section": noise(streams_of[5], (SECTIONS, K, K), (PB * GROUP * K) ** -0.5, 0.09375, ((0, 128),), jnp.float32),
        "down_section": noise(streams_of[6], (SECTIONS, K, K), K ** -0.5, 0.75, ((0, 128),), jnp.float32),
        "section_coupling": noise(streams_of[7], (SECTIONS, C1, K, K), (C1 * K) ** -0.5, 0.25, ((0, 128),), jnp.float32),
        "top_coupling": noise(streams_of[8], (TOPS, C2, K, K), (C2 * K) ** -0.5, 0.25, ((0, 4),), jnp.float32),
        "near_blocks": noise(streams_of[9], (NEAR, P_SIZE, P_SIZE), (NEAR * P_SIZE) ** -0.5, 0.125),
        "leaf_parent": draw_leaf_parent(jax.random.fold_in(streams_of[14], 71), 0),
        "near_list": draw_near_list(jax.random.fold_in(streams_of[14], 71), 0),
        "section_list": draw_section_list(jax.random.fold_in(streams_of[14], 71), 0),
        "top_list": draw_top_list(jax.random.fold_in(streams_of[14], 71), 0),
    }


def reference(sources, source_basis, target_basis, up_leaf, down_leaf, up_section, down_section, section_coupling, top_coupling, near_blocks, leaf_parent, near_list, section_list, top_list):
    highest = lax.Precision.HIGHEST
    boxes = sources.shape[0]
    sections = up_section.shape[0]
    tops = top_coupling.shape[0]
    leaf_moments = jnp.einsum('brp,bkp->brk', sources.astype(jnp.float32), source_basis.astype(jnp.float32), precision=highest)
    lifted = jnp.einsum('brk,bkl->brl', leaf_moments, up_leaf, precision=highest)
    section_moments = jax.ops.segment_sum(lifted, leaf_parent, num_segments=sections)
    raised = jnp.einsum('qrk,qkl->qrl', section_moments, up_section, precision=highest)
    top_moments = raised.reshape(tops, sections // tops, R, K).sum(axis=1)
    top_locals = jnp.einsum('tjrk,tjkl->trl', top_moments[top_list], top_coupling, precision=highest)
    spread = jnp.repeat(top_locals, sections // tops, axis=0)
    section_locals = jnp.einsum('qrk,qkl->qrl', spread, down_section, precision=highest)
    section_locals = section_locals + jnp.einsum('qjrk,qjkl->qrl', section_moments[section_list], section_coupling, precision=highest)
    leaf_locals = jnp.einsum('brk,bkl->brl', section_locals[leaf_parent], down_leaf, precision=highest).astype(jnp.bfloat16)
    far_field = jnp.einsum('brk,bkp->brp', leaf_locals.astype(jnp.float32), target_basis.astype(jnp.float32), precision=highest)
    near_field = jnp.zeros((boxes * R, P_SIZE), jnp.float32)
    for entry in range(NEAR):
        picked = sources[near_list[:, entry]].reshape(boxes * R, P_SIZE)
        near_field = near_field + jnp.dot(picked, near_blocks[entry], preferred_element_type=jnp.float32)
    return (far_field + near_field.reshape(boxes, R, P_SIZE)).astype(jnp.bfloat16)
```

```python
import jax
import jax.numpy as jnp
from jax import lax
from jax.experimental import pallas as pl
from jax.experimental.pallas import tpu as pltpu
from jax.sharding import PartitionSpec as P

GROUP = 4
F32 = jnp.float32
BF16 = jnp.bfloat16
VMEM_LIMIT = 64 * 1024 * 1024
ANY = pl.BlockSpec(memory_space=pl.ANY)
SMEM = pl.BlockSpec(memory_space=pltpu.SMEM)


def dot(a, b):
    return jnp.dot(a, b, preferred_element_type=F32)


def split(x):
    hi = x.astype(BF16)
    return hi, (x - hi.astype(F32)).astype(BF16)


def dot_split(x, w):
    rows = x.shape[0]
    hi, lo = split(x)
    w_hi, w_lo = split(w)
    both = dot(jnp.concatenate([hi, lo], axis=0), w_hi)
    return both[:rows] + both[rows:] + dot(hi, w_lo)


def own_mask(rhs, rank):
    row = lax.broadcasted_iota(jnp.int32, (4 * rhs, 4 * rank), 0) // rhs
    col = lax.broadcasted_iota(jnp.int32, (4 * rhs, 4 * rank), 1) // rank
    return row == col


def moments_kernel(
    parent, sources, source_basis, up_leaf, up_section, pack, top,
    src, basis, lift, raise_, total, out, sems, out_sems,
):
    count, rhs, points = src.shape
    rank = basis.shape[1]
    sections = total.shape[0]
    chunks = 4
    boxes = count // chunks
    keep = pltpu.make_async_copy(src, pack.at[pl.ds(0, count)], out_sems.at[0])
    copies = []
    for c in range(chunks):
        at = pl.ds(c * boxes, boxes)
        copies.append(
            [
                pltpu.make_async_copy(ref.at[at], buf.at[at], sems.at[3 * c + k])
                for k, (ref, buf) in enumerate(((sources, src), (source_basis, basis), (up_leaf, lift)))
            ]
        )
    last = pltpu.make_async_copy(up_section, raise_, sems.at[3 * chunks])
    for group in copies:
        for copy in group:
            copy.start()
    last.start()
    total[...] = jnp.zeros_like(total)
    own = own_mask(rhs, rank)
    for c in range(chunks):
        for copy in copies[c]:
            copy.wait()
        parts = [slice(c * boxes + 4 * f, c * boxes + 4 * f + 4) for f in range(boxes // 4)]
        crossed = [
            lax.dot_general(
                src[part].reshape(4 * rhs, points),
                basis[part].reshape(4 * rank, points),
                (((1,), (1,)), ((), ())),
                preferred_element_type=F32,
            )
            for part in parts
        ]
        lifted = [
            dot_split(jnp.where(own, x, 0.0), lift[part].reshape(4 * rank, rank))
            for x, part in zip(crossed, parts)
        ]
        for f, x in enumerate(lifted):
            for one in range(4):
                slot = parent[c * boxes + 4 * f + one] % sections
                total[slot] += x[one * rhs : (one + 1) * rhs]
    keep.start()
    last.wait()
    for four in range(sections // 4):
        wide = jnp.concatenate([total[4 * four + one] for one in range(4)], axis=1)
        out[four] = wide.astype(BF16)
        term = dot_split(wide, raise_[4 * four : 4 * four + 4].reshape(4 * rank, rank))
        partial = term if four == 0 else partial + term
    half = rhs // 2
    packed = jnp.concatenate([partial[:half], partial[half:]], axis=1).astype(BF16)
    top[...] = jnp.broadcast_to(packed[None], top.shape)
    tail = pltpu.make_async_copy(out, pack.at[pl.ds(count, sections // 4)], out_sems.at[1])
    tail.start()
    tail.wait()
    keep.wait()


def moments_call(parent, sources, source_basis, up_leaf, up_section, devices):
    count, rhs, points = sources.shape
    rank = source_basis.shape[1]
    sections = up_section.shape[0]
    return pl.pallas_call(
        moments_kernel,
        in_specs=[SMEM, ANY, ANY, ANY, ANY],
        out_specs=[ANY, pl.BlockSpec(memory_space=pltpu.VMEM)],
        out_shape=[
            jax.ShapeDtypeStruct((count + sections // 4, rhs, points), BF16),
            jax.ShapeDtypeStruct((devices, rhs // 2, 2 * rank), BF16),
        ],
        scratch_shapes=[
            pltpu.VMEM(sources.shape, BF16),
            pltpu.VMEM(source_basis.shape, BF16),
            pltpu.VMEM(up_leaf.shape, F32),
            pltpu.VMEM(up_section.shape, F32),
            pltpu.VMEM((sections, rhs, rank), F32),
            pltpu.VMEM((sections // 4, rhs, 4 * rank), BF16),
            pltpu.SemaphoreType.DMA((13,)),
            pltpu.SemaphoreType.DMA((2,)),
        ],
        compiler_params=pltpu.CompilerParams(vmem_limit_bytes=VMEM_LIMIT),
        cost_estimate=pl.CostEstimate(flops=0, bytes_accessed=0, transcendentals=0),
        name="moments",
    )(parent, sources, source_basis, up_leaf, up_section)


def coupled_kernel(
    slots, low, high, coupling, out,
    beside, weights, left, right, sems,
):
    sections, rhs, rank = out.shape
    links = coupling.shape[1]
    fours = sections // 4
    count = low.shape[0] - fours
    near = [
        pltpu.make_async_copy(ref.at[pl.ds(count, fours)], beside.at[k], sems.at[k])
        for k, ref in enumerate((low, high))
    ]
    chunks = 4
    here = sections // chunks
    loads = [
        pltpu.make_async_copy(
            coupling.at[pl.ds(c * here, here)], weights.at[pl.ds(c * here, here)], sems.at[2 + c]
        )
        for c in range(chunks)
    ]
    for copy in near + loads:
        copy.start()
    for copy in near:
        copy.wait()
    zero = jnp.zeros((rhs, rank), F32)
    for side in range(2):
        for four in range(fours):
            wide = beside[side, four].astype(F32)
            for one in range(4):
                value = wide[:, one * rank : (one + 1) * rank]
                at = side * sections + 4 * four + one
                left[at] = jnp.concatenate([value, zero], axis=1).astype(BF16)
                right[at] = jnp.concatenate([zero, value], axis=1).astype(BF16)
    for c in range(chunks):
        loads[c].wait()
        for q in range(c * here, (c + 1) * here):
            pairs = [
                left[slots[q * links + j]] + right[slots[q * links + j + 1]]
                for j in range(0, links, 2)
            ]
            wide = jnp.concatenate(pairs, axis=1)
            out[q] = dot(wide, weights[q].reshape(links * rank, rank).astype(BF16))


def coupled_call(slots, low, high, coupling):
    sections, links, rank = coupling.shape[:3]
    rhs, points = low.shape[1:]
    vmem = pl.BlockSpec(memory_space=pltpu.VMEM)
    return pl.pallas_call(
        coupled_kernel,
        in_specs=[SMEM, ANY, ANY, ANY],
        out_specs=vmem,
        out_shape=jax.ShapeDtypeStruct((sections, rhs, rank), F32),
        scratch_shapes=[
            pltpu.VMEM((2, sections // 4, rhs, points), BF16),
            pltpu.VMEM(coupling.shape, F32),
            pltpu.VMEM((2 * sections, rhs, 2 * rank), BF16),
            pltpu.VMEM((2 * sections, rhs, 2 * rank), BF16),
            pltpu.SemaphoreType.DMA((6,)),
        ],
        compiler_params=pltpu.CompilerParams(vmem_limit_bytes=VMEM_LIMIT),
        cost_estimate=pl.CostEstimate(flops=0, bytes_accessed=0, transcendentals=0),
        name="coupled",
    )(slots, low, high, coupling)


def far_kernel(
    parent, links, tops, couplers, down_section, coupled, down_leaf, target, out,
    tops_v, coupler, section_w, coupled_v, leaf_w, target_w, tables, spread, sems,
):
    count, rank, points = target.shape
    sections, rhs, _ = coupled.shape
    link_count = coupler.shape[0]
    slabs = 4
    pairs = (
        (tops, tops_v), (couplers.at[links[0]], coupler), (down_section, section_w),
        (coupled, coupled_v), (down_leaf, leaf_w), (target, target_w),
    )
    loads = [pltpu.make_async_copy(ref, buf, sems.at[k]) for k, (ref, buf) in enumerate(pairs)]
    for copy in loads:
        copy.start()

    for copy in loads[:4]:
        copy.wait()
    half = rhs // 2
    lane = lax.broadcasted_iota(jnp.int32, (half, 2 * rank), 1) < rank
    sums = []
    for j in range(link_count):
        link = links[1 + j]
        first = (link % 8) * (4 * slabs) + link // 8
        total = tops_v[first].astype(F32)
        for one in range(1, 4):
            total += tops_v[first + one * slabs].astype(F32)
        sums.append(total)
    wide = []
    for j in range(0, link_count, 2):
        upper = jnp.where(lane, sums[j], pltpu.roll(sums[j + 1], rank, 1))
        lower = jnp.where(lane, pltpu.roll(sums[j], rank, 1), sums[j + 1])
        wide.append(jnp.concatenate([upper, lower], axis=0))
    local = dot_split(jnp.concatenate(wide, axis=1), coupler[...].reshape(link_count * rank, rank))
    zero = jnp.zeros((rhs, rank), F32)
    for q in range(sections):
        value = dot_split(local, section_w[q]) + coupled_v[q]
        tables[0, q], tables[1, q] = split(jnp.concatenate([value, zero], axis=1))
        tables[2, q], tables[3, q] = split(jnp.concatenate([zero, value], axis=1))

    loads[4].wait()
    mask = own_mask(rhs, rank)
    none = jnp.zeros((rhs, 2 * rank), BF16)
    for four in range(count // 4):
        slot = [parent[4 * four + one] % sections for one in range(4)]
        rows = []
        for part in range(2):
            a, b = tables.at[part], tables.at[2 + part]
            rows += [
                jnp.concatenate([a[slot[0]], none], axis=1),
                jnp.concatenate([b[slot[1]], none], axis=1),
                jnp.concatenate([none, a[slot[2]]], axis=1),
                jnp.concatenate([none, b[slot[3]]], axis=1),
            ]
        w_hi, w_lo = split(leaf_w[4 * four : 4 * four + 4].reshape(4 * rank, rank))
        both = dot(jnp.concatenate(rows, axis=0), w_hi)
        value = both[: 4 * rhs] + both[4 * rhs :] + dot(jnp.concatenate(rows[:4], axis=0), w_lo)
        double = jnp.concatenate([value, value], axis=1)
        spread[four] = jnp.where(mask, jnp.concatenate([double, double], axis=1), 0.0).astype(BF16)
    loads[5].wait()
    for four in range(count // 4):
        at = pl.ds(4 * four * rhs, 4 * rhs)
        out[at] = dot(spread[four], target_w[4 * four : 4 * four + 4].reshape(4 * rank, points))


def far_call(parent, links, tops, couplers, down_section, coupled, down_leaf, target):
    count, rank, points = target.shape
    sections, rhs, _ = coupled.shape
    return pl.pallas_call(
        far_kernel,
        in_specs=[SMEM] * 2 + [ANY] * 6,
        out_specs=pl.BlockSpec(memory_space=pltpu.VMEM),
        out_shape=jax.ShapeDtypeStruct((count * rhs, points), F32),
        scratch_shapes=[
            pltpu.VMEM(tops.shape, BF16),
            pltpu.VMEM(couplers.shape[1:], F32),
            pltpu.VMEM(down_section.shape, F32),
            pltpu.VMEM(coupled.shape, F32),
            pltpu.VMEM(down_leaf.shape, F32),
            pltpu.VMEM(target.shape, BF16),
            pltpu.VMEM((4, sections, rhs, 2 * rank), BF16),
            pltpu.VMEM((count // 4, 4 * rhs, 4 * rank), BF16),
            pltpu.SemaphoreType.DMA((6,)),
        ],
        compiler_params=pltpu.CompilerParams(vmem_limit_bytes=VMEM_LIMIT),
        cost_estimate=pl.CostEstimate(flops=50_000_000_000, bytes_accessed=6_000_000, transcendentals=0),
        name="far",
    )(parent, links, tops, couplers, down_section, coupled, down_leaf, target)


def near_kernel(
    codes, own_src, left_src, right_src, low_src, high_src, corner_left, corner_right,
    near_blocks, far, out, blocks, wide, near_w, far_v, sems,
):
    count, rhs, points = own_src.shape
    entries = near_blocks.shape[0]
    leaf_rows = pl.ds(0, count)
    places = (
        corner_left.at[0], low_src, corner_right.at[0],
        left_src.at[leaf_rows], own_src, right_src.at[leaf_rows],
        corner_left.at[1], high_src, corner_right.at[1],
    )
    loads = [pltpu.make_async_copy(ref, blocks.at[k], sems.at[k]) for k, ref in enumerate(places)]
    loads.append(pltpu.make_async_copy(near_blocks, near_w, sems.at[9]))
    loads.append(pltpu.make_async_copy(far, far_v, sems.at[10]))
    for copy in loads:
        copy.start()

    for k in range(9):
        loads[k].wait()
        for b in range(count):
            code = codes[k * count + b]
            wide[code // count, pl.ds(b * rhs, rhs)] = blocks[k, code % count]
    loads[9].wait()
    loads[10].wait()
    chunk = 16
    for part in range(count // chunk):
        at = pl.ds(part * chunk * rhs, chunk * rhs)
        total = far_v[at]
        for j in range(entries):
            total += dot(wide[j, at], near_w[j])
        out[pl.ds(part * chunk, chunk)] = total.astype(BF16).reshape(chunk, rhs, points)


def near_call(codes, blocks, near_blocks, far):
    count, rhs, points = blocks[0].shape
    entries = near_blocks.shape[0]
    return pl.pallas_call(
        near_kernel,
        in_specs=[SMEM] + [ANY] * 9,
        out_specs=pl.BlockSpec(memory_space=pltpu.VMEM),
        out_shape=jax.ShapeDtypeStruct((count, rhs, points), BF16),
        scratch_shapes=[
            pltpu.VMEM((9, count, rhs, points), BF16),
            pltpu.VMEM((entries, count * rhs, points), BF16),
            pltpu.VMEM(near_blocks.shape, BF16),
            pltpu.VMEM(far.shape, F32),
            pltpu.SemaphoreType.DMA((11,)),
        ],
        compiler_params=pltpu.CompilerParams(vmem_limit_bytes=VMEM_LIMIT),
        cost_estimate=pl.CostEstimate(flops=1_200_000_000, bytes_accessed=8_000_000, transcendentals=0),
        name="near",
    )(codes, *blocks, near_blocks, far)


def shifted(x, axis, step):
    count = lax.axis_size(axis)
    return lax.ppermute(x, axis, [(i, (i + step) % count) for i in range(count)])


def shards(
    sources, source_basis, target_basis, up_leaf, down_leaf, up_section, down_section,
    section_coupling, top_coupling, near_blocks, leaf_parent, near_list, section_list, top_list,
):
    leaf_count = sources.shape[0]
    section_count = up_section.shape[0]
    leaves = lax.axis_size("leaf")
    slabs = lax.axis_size("slab")
    my_leaf = lax.axis_index("leaf")
    my_slab = lax.axis_index("slab")

    owner = near_list // leaf_count
    rel_slab = (owner // leaves - my_slab + 1) % slabs
    rel_leaf = (owner % leaves - my_leaf + 1) % leaves
    entry = jnp.arange(near_list.shape[1], dtype=jnp.int32)
    code = entry * leaf_count + near_list % leaf_count
    place = rel_slab * 3 + rel_leaf
    found = place[None] == jnp.arange(9, dtype=jnp.int32)[:, None, None]
    codes = jnp.sum(jnp.where(found, code[None], 0), axis=2).reshape(-1)
    side = (section_list // section_count % leaves - my_leaf + 1) % leaves // 2
    side_slot = (side * section_count + section_list % section_count).reshape(-1)
    my_top = my_leaf // GROUP
    links = lax.dynamic_index_in_dim(top_list, my_top, 0, keepdims=False)
    links = jnp.concatenate([my_top[None].astype(jnp.int32), links])

    from_low = shifted(sources, "slab", 1)
    from_high = shifted(sources, "slab", -1)
    pack, sent = moments_call(
        leaf_parent, sources, source_basis, up_leaf, up_section, leaves * slabs
    )
    tops = lax.all_to_all(sent, ("leaf", "slab"), 0, 0, tiled=True)
    left = shifted(pack, "leaf", 1)
    right = shifted(pack, "leaf", -1)
    coupled = coupled_call(side_slot, left, right, section_coupling)
    corners = jnp.stack([from_low, from_high])
    corner_left = shifted(corners, "leaf", 1)
    corner_right = shifted(corners, "leaf", -1)
    far = far_call(
        leaf_parent, links, tops, top_coupling, down_section, coupled, down_leaf, target_basis
    )
    blocks = (sources, left, right, from_low, from_high, corner_left, corner_right)
    return near_call(codes, blocks, near_blocks, far)


def solution(mesh):
    in_specs = (
        P(("slab", "leaf"), None, None),
        P(("slab", "leaf"), None, None),
        P(("slab", "leaf"), None, None),
        P(("slab", "leaf"), None, None),
        P(("slab", "leaf"), None, None),
        P(("slab", "leaf"), None, None),
        P(("slab", "leaf"), None, None),
        P(("slab", "leaf"), None, None, None),
        P("slab", None, None, None),
        P(),
        P(("slab", "leaf")),
        P(("slab", "leaf"), None),
        P(("slab", "leaf"), None),
        P("slab", None),
    )
    out_specs = P(("slab", "leaf"), None, None)
    return jax.shard_map(shards, mesh=mesh, in_specs=in_specs, out_specs=out_specs, check_vma=False)
```

```python
import jax
import jax.numpy as jnp
from jax import lax
from jax.experimental import pallas as pl
from jax.experimental.pallas import tpu as pltpu
from jax.sharding import PartitionSpec as P

GROUP = 4
F32 = jnp.float32
BF16 = jnp.bfloat16
HBM = pl.BlockSpec(memory_space=pltpu.HBM)
VMEM = pl.BlockSpec(memory_space=pltpu.VMEM)
SMEM = pl.BlockSpec(memory_space=pltpu.SMEM)
LISTS = 4
PACK = 32


def params(mib=64):
    return pltpu.CompilerParams(vmem_limit_bytes=mib * 1024 * 1024)


def cost(us):
    return pl.CostEstimate(flops=int(us * 1_000_000_000), bytes_accessed=0, transcendentals=0)


def dot(a, b):
    return jnp.dot(a, b, preferred_element_type=F32)


def split(x):
    hi = x.astype(BF16)
    return hi, (x - hi.astype(F32)).astype(BF16)


def dot_split(x, w):
    rows = x.shape[0]
    hi, lo = split(x)
    w_hi, w_lo = split(w)
    both = dot(jnp.concatenate([hi, lo], axis=0), w_hi)
    return both[:rows] + both[rows:] + dot(hi, w_lo)


def own_mask(rhs, rank):
    row = lax.broadcasted_iota(jnp.int32, (4 * rhs, 4 * rank), 0) // rhs
    col = lax.broadcasted_iota(jnp.int32, (4 * rhs, 4 * rank), 1) // rank
    return row == col


def started(pairs, sems):
    copies = [pltpu.make_async_copy(ref, buf, sems.at[k]) for k, (ref, buf) in enumerate(pairs)]
    for copy in copies:
        copy.start()
    return copies


def list_place(entries, count):
    my_leaf = lax.axis_index("leaf")
    my_slab = lax.axis_index("slab")
    leaves = lax.axis_size("leaf")
    slabs = lax.axis_size("slab")
    owner = entries // count
    rel_slab = (owner // leaves - my_slab + 1) & (slabs - 1)
    rel_leaf = ((owner & (leaves - 1)) - my_leaf + 1) & (leaves - 1)
    return rel_leaf, rel_slab * count + (entries & (count - 1))


def moments_kernel(
    parent, sources, source_basis, up_leaf, up_section, near_list, to_inner, to_outer, top,
    src, basis, lift, raise_, lists, total, sems,
):
    count, rhs, points = src.shape
    rank = basis.shape[1]
    sections = total.shape[0]
    chunks = 4
    boxes = count // chunks
    pairs = []
    for c in range(chunks):
        at = pl.ds(c * boxes, boxes)
        pairs += [(ref.at[at], buf.at[at]) for ref, buf in ((sources, src), (source_basis, basis), (up_leaf, lift))]
        if c == 0:
            pairs += [(near_list, lists), (up_section, raise_)]
    copies = started(pairs, sems)
    total[...] = jnp.zeros_like(total)
    to_inner[...] = jnp.zeros_like(to_inner)
    to_outer[...] = jnp.zeros_like(to_outer)
    own = own_mask(rhs, rank)
    at_copy = 0
    for c in range(chunks):
        many = 5 if c == 0 else 3
        for copy in copies[at_copy : at_copy + many]:
            copy.wait()
        at_copy += many
        parts = [slice(c * boxes + 4 * f, c * boxes + 4 * f + 4) for f in range(boxes // 4)]
        crossed = [
            lax.dot_general(
                src[part].reshape(4 * rhs, points),
                basis[part].reshape(4 * rank, points),
                (((1,), (1,)), ((), ())),
                preferred_element_type=F32,
            )
            for part in parts
        ]
        lifted = [
            dot_split(jnp.where(own, x, 0.0), lift[part].reshape(4 * rank, rank))
            for x, part in zip(crossed, parts)
        ]
        for f, x in enumerate(lifted):
            for one in range(4):
                slot = parent[c * boxes + 4 * f + one] & (sections - 1)
                total[slot] += x[one * rhs : (one + 1) * rhs]
    fours = sections // 4
    for four in range(fours):
        wide = jnp.concatenate([total[4 * four + one] for one in range(4)], axis=1)
        to_inner[four] = wide.astype(BF16)
        to_outer[four] = wide.astype(BF16)
        term = dot_split(wide, raise_[4 * four : 4 * four + 4].reshape(4 * rank, rank))
        partial = term if four == 0 else partial + term
    half = rhs // 2
    packed = jnp.concatenate([partial[:half], partial[half:]], axis=1).astype(BF16)
    top[...] = jnp.broadcast_to(packed[None], top.shape)

    entries = lists[...]
    rel_leaf, place = list_place(entries, count)
    rows, boxes = entries.shape
    odd = lax.axis_index("leaf") & 1
    for ref, step in ((to_inner, 2 - 2 * odd), (to_outer, 2 * odd)):
        ref[fours, :rows, :boxes] = jnp.where(rel_leaf == step, place, 3 * count).astype(F32).astype(BF16)


def moments_call(parent, sources, source_basis, up_leaf, up_section, near_list, devices):
    count, rhs, points = sources.shape
    rank = source_basis.shape[1]
    sections = up_section.shape[0]
    pack = jax.ShapeDtypeStruct((PACK, rhs, points), BF16)
    return pl.pallas_call(
        moments_kernel,
        in_specs=[SMEM, HBM, HBM, HBM, HBM, HBM],
        out_specs=[VMEM, VMEM, VMEM],
        out_shape=[pack, pack, jax.ShapeDtypeStruct((devices, rhs // 2, 2 * rank), BF16)],
        scratch_shapes=[
            pltpu.VMEM(sources.shape, BF16),
            pltpu.VMEM(source_basis.shape, BF16),
            pltpu.VMEM(up_leaf.shape, F32),
            pltpu.VMEM(up_section.shape, F32),
            pltpu.VMEM(near_list.shape, jnp.int32),
            pltpu.VMEM((sections, rhs, rank), F32),
            pltpu.SemaphoreType.DMA((14,)),
        ],
        compiler_params=params(),
        cost_estimate=cost(0),
        name="moments",
    )(parent, sources, source_basis, up_leaf, up_section, near_list)


def near_sum(codes, table, near_blocks, store):
    entries = near_blocks.shape[0]
    count = 64
    chunk = 16
    for part in range(count // chunk):
        for j in range(entries):
            rows = jnp.concatenate([table[codes(j, part * chunk + b)] for b in range(chunk)], axis=0)
            term = dot(rows, near_blocks[j])
            total = term if j == 0 else total + term
        store(part * chunk, chunk, total)


def beside_kernel(
    inner, outer, from_low, own_src, from_high, near_list, near_blocks,
    to_inner, to_outer, own_codes, table, near_w, lists, entries, coded, codes, sems, code_sems,
):
    count, rhs, points = own_src.shape
    fours = LISTS
    copies = started(
        (
            (inner.at[fours], lists.at[0]), (outer.at[fours], lists.at[1]), (near_list, entries),
            (near_blocks, near_w),
            (from_low, table.at[pl.ds(0, count)]),
            (own_src, table.at[pl.ds(count, count)]),
            (from_high, table.at[pl.ds(2 * count, count)]),
        ),
        sems,
    )
    table[3 * count] = jnp.zeros((rhs, points), BF16)
    for copy in copies[:3]:
        copy.wait()
    rel_leaf, place = list_place(entries[...], count)
    own_codes[...] = jnp.where(rel_leaf == 1, place, 3 * count)
    for k in range(2):
        coded[k] = lists[k].astype(F32).astype(jnp.int32)[:, :128]
    moves = [pltpu.make_async_copy(coded.at[k], codes.at[k], code_sems.at[k]) for k in range(2)]
    for move in moves:
        move.start()
    for copy in copies[3:]:
        copy.wait()
    for move in moves:
        move.wait()
    for k, out in enumerate((to_inner, to_outer)):
        def store(at, many, total, out=out):
            out[pl.ds(at, many)] = total.astype(BF16).reshape(many, rhs, points)

        near_sum(lambda j, b, k=k: codes[k, j, b], table, near_w, store)


def beside_call(inner, outer, from_low, own_src, from_high, near_list, near_blocks):
    count, rhs, points = own_src.shape
    block = jax.ShapeDtypeStruct(own_src.shape, BF16)
    return pl.pallas_call(
        beside_kernel,
        in_specs=[HBM] * 7,
        out_specs=[VMEM] * 3,
        out_shape=[block, block, jax.ShapeDtypeStruct(near_list.shape, jnp.int32)],
        scratch_shapes=[
            pltpu.VMEM((3 * count + 1, rhs, points), BF16),
            pltpu.VMEM(near_blocks.shape, BF16),
            pltpu.VMEM((2, rhs, points), BF16),
            pltpu.VMEM(near_list.shape, jnp.int32),
            pltpu.VMEM((2, rhs, 128), jnp.int32),
            pltpu.SMEM((2, rhs, 128), jnp.int32),
            pltpu.SemaphoreType.DMA((7,)),
            pltpu.SemaphoreType.DMA((2,)),
        ],
        compiler_params=params(),
        cost_estimate=cost(0),
        name="beside",
    )(inner, outer, from_low, own_src, from_high, near_list, near_blocks)


def local_kernel(
    parent, top_links, links, codes,
    inner, outer, coupling, from_low, own_src, from_high, near_blocks, tops, couplers, down_section,
    down_leaf, target, out,
    table, near_w, beside, couple_w, tops_v, coupler, section_w, leaf_w, target_w,
    left, right, coupled, tables, spread, sems,
):
    count, rhs, points = out.shape
    rank = target.shape[1]
    sections, link_count = coupling.shape[:2]
    fours = sections // 4
    my_leaf = lax.axis_index("leaf")
    leaves = lax.axis_size("leaf")
    slabs = lax.axis_size("slab")
    my_top = my_leaf // GROUP
    chunks = 4
    here = sections // chunks
    pairs = [(inner.at[pl.ds(0, fours)], beside.at[0]), (outer.at[pl.ds(0, fours)], beside.at[1])]
    for c in range(chunks):
        at = pl.ds(c * here, here)
        pairs.append((coupling.at[at], couple_w.at[at]))
    pairs += [
        (near_blocks, near_w),
        (from_low, table.at[pl.ds(0, count)]),
        (own_src, table.at[pl.ds(count, count)]),
        (from_high, table.at[pl.ds(2 * count, count)]),
        (tops, tops_v), (couplers.at[my_top], coupler), (down_section, section_w),
        (down_leaf, leaf_w), (target, target_w),
    ]
    copies = started(pairs, sems)

    table[3 * count] = jnp.zeros((rhs, points), BF16)

    for copy in copies[:2]:
        copy.wait()
    zero = jnp.zeros((rhs, rank), F32)
    for side in range(2):
        for four in range(fours):
            wide = beside[side, four].astype(F32)
            for one in range(4):
                value = wide[:, one * rank : (one + 1) * rank]
                at = side * sections + 4 * four + one
                left[at] = jnp.concatenate([value, zero], axis=1).astype(BF16)
                right[at] = jnp.concatenate([zero, value], axis=1).astype(BF16)

    def slot(j, q):
        entry = links[j, q]
        leaf = (entry // sections) & (leaves - 1)
        return jnp.where(leaf == my_leaf ^ 1, 0, sections) + (entry & (sections - 1))

    for q in range(sections):
        if q % here == 0:
            copies[2 + q // here].wait()
        pairs = [left[slot(j, q)] + right[slot(j + 1, q)] for j in range(0, link_count, 2)]
        wide = jnp.concatenate(pairs, axis=1)
        coupled[q] = dot(wide, couple_w[q].reshape(link_count * rank, rank).astype(BF16))

    for copy in copies[6:10]:
        copy.wait()

    def store(at, many, total):
        out[pl.ds(at, many)] = total.reshape(many, rhs, points)

    near_sum(lambda j, b: codes[j, b], table, near_w, store)

    for copy in copies[10:13]:
        copy.wait()
    slab_tops = top_links.shape[0]
    half = rhs // 2
    lane = lax.broadcasted_iota(jnp.int32, (half, 2 * rank), 1) < rank
    sums = []
    for j in range(link_count):
        link = top_links[my_top, j]
        first = (link & (slab_tops - 1)) * (GROUP * slabs) + link // slab_tops
        sums.append(sum(tops_v[first + one * slabs].astype(F32) for one in range(GROUP)))
    wide = []
    for j in range(0, link_count, 2):
        upper = jnp.where(lane, sums[j], pltpu.roll(sums[j + 1], rank, 1))
        lower = jnp.where(lane, pltpu.roll(sums[j], rank, 1), sums[j + 1])
        wide.append(jnp.concatenate([upper, lower], axis=0))
    local = dot_split(jnp.concatenate(wide, axis=1), coupler[...].reshape(link_count * rank, rank))
    for q in range(sections):
        value = dot_split(local, section_w[q]) + coupled[q]
        tables[0, q], tables[1, q] = split(jnp.concatenate([value, zero], axis=1))
        tables[2, q], tables[3, q] = split(jnp.concatenate([zero, value], axis=1))

    for copy in copies[13:]:
        copy.wait()
    mask = own_mask(rhs, rank)
    none = jnp.zeros((rhs, 2 * rank), BF16)
    for four in range(count // 4):
        slots = [parent[4 * four + one] & (sections - 1) for one in range(4)]
        lines = []
        for part in range(2):
            a, b = tables.at[part], tables.at[2 + part]
            lines += [
                jnp.concatenate([a[slots[0]], none], axis=1),
                jnp.concatenate([b[slots[1]], none], axis=1),
                jnp.concatenate([none, a[slots[2]]], axis=1),
                jnp.concatenate([none, b[slots[3]]], axis=1),
            ]
        w_hi, w_lo = split(leaf_w[4 * four : 4 * four + 4].reshape(4 * rank, rank))
        both = dot(jnp.concatenate(lines, axis=0), w_hi)
        value = both[: 4 * rhs] + both[4 * rhs :] + dot(jnp.concatenate(lines[:4], axis=0), w_lo)
        double = jnp.concatenate([value, value], axis=1)
        spread[four] = jnp.where(mask, jnp.concatenate([double, double], axis=1), 0.0).astype(BF16)
    for four in range(count // 4):
        at = pl.ds(4 * four, 4)
        far = dot(spread[four], target_w[4 * four : 4 * four + 4].reshape(4 * rank, points))
        out[at] += far.reshape(4, rhs, points)


def local_call(
    parent, top_links, links, codes, inner, outer, coupling, from_low, own_src, from_high, near_blocks,
    tops, couplers, down_section, down_leaf, target,
):
    rhs = own_src.shape[1]
    count, rank, points = target.shape
    sections = coupling.shape[0]
    return pl.pallas_call(
        local_kernel,
        in_specs=[SMEM] * 4 + [HBM] * 12,
        out_specs=VMEM,
        out_shape=jax.ShapeDtypeStruct((count, rhs, points), F32),
        scratch_shapes=[
            pltpu.VMEM((3 * count + 1, rhs, points), BF16),
            pltpu.VMEM(near_blocks.shape, BF16),
            pltpu.VMEM((2, sections // 4, rhs, points), BF16),
            pltpu.VMEM(coupling.shape, F32),
            pltpu.VMEM(tops.shape, BF16),
            pltpu.VMEM(couplers.shape[1:], F32),
            pltpu.VMEM(down_section.shape, F32),
            pltpu.VMEM(down_leaf.shape, F32),
            pltpu.VMEM(target.shape, BF16),
            pltpu.VMEM((2 * sections, rhs, 2 * rank), BF16),
            pltpu.VMEM((2 * sections, rhs, 2 * rank), BF16),
            pltpu.VMEM((sections, rhs, rank), F32),
            pltpu.VMEM((4, sections, rhs, 2 * rank), BF16),
            pltpu.VMEM((count // 4, 4 * rhs, 4 * rank), BF16),
            pltpu.SemaphoreType.DMA((15,)),
        ],
        compiler_params=params(),
        cost_estimate=cost(40),
        name="local",
    )(
        parent, top_links, links, codes, inner, outer, coupling, from_low, own_src, from_high, near_blocks,
        tops, couplers, down_section, down_leaf, target,
    )


def shifted(x, axis, step):
    count = lax.axis_size(axis)
    return lax.ppermute(x, axis, [(i, (i + step) % count) for i in range(count)])


def swapped(x, first):
    count = lax.axis_size("leaf")
    return lax.ppermute(
        x, "leaf", [(i, (i + (1 if i % 2 == first else -1)) % count) for i in range(count)]
    )


def shards(
    sources, source_basis, target_basis, up_leaf, down_leaf, up_section, down_section,
    section_coupling, top_coupling, near_blocks, leaf_parent, near_list, section_list, top_list,
):
    devices = lax.axis_size("leaf") * lax.axis_size("slab")
    near_list = near_list.T
    from_low = shifted(sources, "slab", 1)
    from_high = shifted(sources, "slab", -1)
    to_inner, to_outer, sent = moments_call(
        leaf_parent, sources, source_basis, up_leaf, up_section, near_list, devices
    )
    inner = swapped(to_inner, 0)
    outer = swapped(to_outer, 1)
    tops = lax.all_to_all(sent, ("leaf", "slab"), 0, 0, tiled=True)
    near_inner, near_outer, codes = beside_call(
        inner, outer, from_low, sources, from_high, near_list, near_blocks
    )
    near_inner = swapped(near_inner, 0)
    near_outer = swapped(near_outer, 1)
    local = local_call(
        leaf_parent, top_list, section_list.T, codes, inner, outer, section_coupling, from_low, sources,
        from_high, near_blocks, tops, top_coupling, down_section, down_leaf, target_basis,
    )
    return (local + near_inner.astype(F32) + near_outer.astype(F32)).astype(BF16)


def solution(mesh):
    in_specs = (
        P(("slab", "leaf"), None, None),
        P(("slab", "leaf"), None, None),
        P(("slab", "leaf"), None, None),
        P(("slab", "leaf"), None, None),
        P(("slab", "leaf"), None, None),
        P(("slab", "leaf"), None, None),
        P(("slab", "leaf"), None, None),
        P(("slab", "leaf"), None, None, None),
        P("slab", None, None, None),
        P(),
        P(("slab", "leaf")),
        P(("slab", "leaf"), None),
        P(("slab", "leaf"), None),
        P("slab", None),
    )
    out_specs = P(("slab", "leaf"), None, None)
    return jax.shard_map(shards, mesh=mesh, in_specs=in_specs, out_specs=out_specs, check_vma=False)
```

```python
import jax
import jax.numpy as jnp
from jax import lax
from jax.experimental import pallas as pl
from jax.experimental.pallas import tpu as pltpu
from jax.sharding import PartitionSpec as P

GROUP = 4
F32 = jnp.float32
BF16 = jnp.bfloat16
HBM = pl.BlockSpec(memory_space=pltpu.HBM)
VMEM = pl.BlockSpec(memory_space=pltpu.VMEM)
SMEM = pl.BlockSpec(memory_space=pltpu.SMEM)
LISTS = 4
PACK = 32


def params(mib=64):
    return pltpu.CompilerParams(vmem_limit_bytes=mib * 1024 * 1024)


def cost(us):
    return pl.CostEstimate(flops=int(us * 1_000_000_000), bytes_accessed=0, transcendentals=0)


def dot(a, b):
    return jnp.dot(a, b, preferred_element_type=F32)


def split(x):
    hi = x.astype(BF16)
    return hi, (x - hi.astype(F32)).astype(BF16)


def dot_split(x, w):
    rows = x.shape[0]
    hi, lo = split(x)
    w_hi, w_lo = split(w)
    both = dot(jnp.concatenate([hi, lo], axis=0), w_hi)
    return both[:rows] + both[rows:] + dot(hi, w_lo)


def own_mask(rhs, rank):
    row = lax.broadcasted_iota(jnp.int32, (4 * rhs, 4 * rank), 0) // rhs
    col = lax.broadcasted_iota(jnp.int32, (4 * rhs, 4 * rank), 1) // rank
    return row == col


def started(pairs, sems):
    copies = [pltpu.make_async_copy(ref, buf, sems.at[k]) for k, (ref, buf) in enumerate(pairs)]
    for copy in copies:
        copy.start()
    return copies


def list_place(entries, count):
    my_leaf = lax.axis_index("leaf")
    my_slab = lax.axis_index("slab")
    leaves = lax.axis_size("leaf")
    slabs = lax.axis_size("slab")
    owner = entries // count
    rel_slab = (owner // leaves - my_slab + 1) & (slabs - 1)
    rel_leaf = ((owner & (leaves - 1)) - my_leaf + 1) & (leaves - 1)
    return rel_leaf, rel_slab * count + (entries & (count - 1))


def moments_kernel(
    parent, sources, source_basis, up_leaf, up_section, near_list, to_inner, to_outer, top,
    src, basis, lift, raise_, lists, total, sems,
):
    count, rhs, points = src.shape
    rank = basis.shape[1]
    sections = total.shape[0]
    chunks = 2
    boxes = count // chunks
    pairs = []
    for c in range(chunks):
        at = pl.ds(c * boxes, boxes)
        pairs += [(ref.at[at], buf.at[at]) for ref, buf in ((sources, src), (source_basis, basis), (up_leaf, lift))]
        if c == 0:
            pairs += [(near_list, lists), (up_section, raise_)]
    copies = started(pairs, sems)
    total[...] = jnp.zeros_like(total)
    to_inner[...] = jnp.zeros_like(to_inner)
    to_outer[...] = jnp.zeros_like(to_outer)
    own = own_mask(rhs, rank)
    at_copy = 0
    for c in range(chunks):
        many = 5 if c == 0 else 3
        for copy in copies[at_copy : at_copy + many]:
            copy.wait()
        at_copy += many
        parts = [slice(c * boxes + 4 * f, c * boxes + 4 * f + 4) for f in range(boxes // 4)]
        crossed = [
            lax.dot_general(
                src[part].reshape(4 * rhs, points),
                basis[part].reshape(4 * rank, points),
                (((1,), (1,)), ((), ())),
                preferred_element_type=F32,
            )
            for part in parts
        ]
        lifted = [
            dot_split(jnp.where(own, x, 0.0), lift[part].reshape(4 * rank, rank))
            for x, part in zip(crossed, parts)
        ]
        for f, x in enumerate(lifted):
            for one in range(4):
                slot = parent[c * boxes + 4 * f + one] & (sections - 1)
                total[slot] += x[one * rhs : (one + 1) * rhs]
    fours = sections // 4
    for four in range(fours):
        wide = jnp.concatenate([total[4 * four + one] for one in range(4)], axis=1)
        to_inner[four] = wide.astype(BF16)
        to_outer[four] = wide.astype(BF16)
        term = dot_split(wide, raise_[4 * four : 4 * four + 4].reshape(4 * rank, rank))
        partial = term if four == 0 else partial + term
    half = rhs // 2
    packed = jnp.concatenate([partial[:half], partial[half:]], axis=1).astype(BF16)
    top[...] = jnp.broadcast_to(packed[None], top.shape)

    entries = lists[...]
    rel_leaf, place = list_place(entries, count)
    rows, boxes = entries.shape
    odd = lax.axis_index("leaf") & 1
    for ref, step in ((to_inner, 2 - 2 * odd), (to_outer, 2 * odd)):
        ref[fours, :rows, :boxes] = jnp.where(rel_leaf == step, place, 3 * count).astype(F32).astype(BF16)


def moments_call(parent, sources, source_basis, up_leaf, up_section, near_list, devices):
    count, rhs, points = sources.shape
    rank = source_basis.shape[1]
    sections = up_section.shape[0]
    pack = jax.ShapeDtypeStruct((PACK, rhs, points), BF16)
    return pl.pallas_call(
        moments_kernel,
        in_specs=[SMEM, HBM, HBM, HBM, HBM, HBM],
        out_specs=[VMEM, VMEM, VMEM],
        out_shape=[pack, pack, jax.ShapeDtypeStruct((devices, rhs // 2, 2 * rank), BF16)],
        scratch_shapes=[
            pltpu.VMEM(sources.shape, BF16),
            pltpu.VMEM(source_basis.shape, BF16),
            pltpu.VMEM(up_leaf.shape, F32),
            pltpu.VMEM(up_section.shape, F32),
            pltpu.VMEM(near_list.shape, jnp.int32),
            pltpu.VMEM((sections, rhs, rank), F32),
            pltpu.SemaphoreType.DMA((14,)),
        ],
        compiler_params=params(),
        cost_estimate=cost(0),
        name="moments",
    )(parent, sources, source_basis, up_leaf, up_section, near_list)


def near_sum(codes, table, near_blocks, store):
    entries = near_blocks.shape[0]
    count = 64
    chunk = 16
    for part in range(count // chunk):
        for j in range(entries):
            rows = jnp.concatenate([table[codes(j, part * chunk + b)] for b in range(chunk)], axis=0)
            term = dot(rows, near_blocks[j])
            total = term if j == 0 else total + term
        store(part * chunk, chunk, total)


def beside_kernel(
    inner, outer, from_low, own_src, from_high, near_list, near_blocks,
    to_inner, to_outer, own_codes, table, near_w, lists, entries, coded, codes, sems, code_sems,
):
    count, rhs, points = own_src.shape
    fours = LISTS
    copies = started(
        (
            (inner.at[fours], lists.at[0]), (outer.at[fours], lists.at[1]), (near_list, entries),
            (near_blocks, near_w),
            (from_low, table.at[pl.ds(0, count)]),
            (own_src, table.at[pl.ds(count, count)]),
            (from_high, table.at[pl.ds(2 * count, count)]),
        ),
        sems,
    )
    table[3 * count] = jnp.zeros((rhs, points), BF16)
    for copy in copies[:3]:
        copy.wait()
    rel_leaf, place = list_place(entries[...], count)
    own_codes[...] = jnp.where(rel_leaf == 1, place, 3 * count)
    for k in range(2):
        coded[k] = lists[k].astype(F32).astype(jnp.int32)[:, :128]
    moves = [pltpu.make_async_copy(coded.at[k], codes.at[k], code_sems.at[k]) for k in range(2)]
    for move in moves:
        move.start()
    for copy in copies[3:]:
        copy.wait()
    for move in moves:
        move.wait()
    for k, out in enumerate((to_inner, to_outer)):
        def store(at, many, total, out=out):
            out[pl.ds(at, many)] = total.astype(BF16).reshape(many, rhs, points)

        near_sum(lambda j, b, k=k: codes[k, j, b], table, near_w, store)


def beside_call(inner, outer, from_low, own_src, from_high, near_list, near_blocks):
    count, rhs, points = own_src.shape
    block = jax.ShapeDtypeStruct(own_src.shape, BF16)
    return pl.pallas_call(
        beside_kernel,
        in_specs=[HBM] * 7,
        out_specs=[VMEM] * 3,
        out_shape=[block, block, jax.ShapeDtypeStruct(near_list.shape, jnp.int32)],
        scratch_shapes=[
            pltpu.VMEM((3 * count + 1, rhs, points), BF16),
            pltpu.VMEM(near_blocks.shape, BF16),
            pltpu.VMEM((2, rhs, points), BF16),
            pltpu.VMEM(near_list.shape, jnp.int32),
            pltpu.VMEM((2, rhs, 128), jnp.int32),
            pltpu.SMEM((2, rhs, 128), jnp.int32),
            pltpu.SemaphoreType.DMA((7,)),
            pltpu.SemaphoreType.DMA((2,)),
        ],
        compiler_params=params(),
        cost_estimate=cost(0),
        name="beside",
    )(inner, outer, from_low, own_src, from_high, near_list, near_blocks)


def local_kernel(
    parent, top_links, links, codes,
    inner, outer, coupling, from_low, own_src, from_high, near_blocks, tops, couplers, down_section,
    down_leaf, target, out,
    table, near_w, beside, couple_w, tops_v, coupler, section_w, leaf_w, target_w,
    left, right, coupled, tables, spread, sems,
):
    count, rhs, points = out.shape
    rank = target.shape[1]
    sections, link_count = coupling.shape[:2]
    fours = sections // 4
    my_leaf = lax.axis_index("leaf")
    leaves = lax.axis_size("leaf")
    slabs = lax.axis_size("slab")
    my_top = my_leaf // GROUP
    chunks = 2
    here = sections // chunks
    pairs = [(inner.at[pl.ds(0, fours)], beside.at[0]), (outer.at[pl.ds(0, fours)], beside.at[1])]
    for c in range(chunks):
        at = pl.ds(c * here, here)
        pairs.append((coupling.at[at], couple_w.at[at]))
    pairs += [
        (near_blocks, near_w),
        (from_low, table.at[pl.ds(0, count)]),
        (own_src, table.at[pl.ds(count, count)]),
        (from_high, table.at[pl.ds(2 * count, count)]),
        (tops, tops_v), (couplers.at[my_top], coupler), (down_section, section_w),
        (down_leaf, leaf_w), (target, target_w),
    ]
    copies = started(pairs, sems)

    table[3 * count] = jnp.zeros((rhs, points), BF16)

    for copy in copies[:2]:
        copy.wait()
    zero = jnp.zeros((rhs, rank), F32)
    for side in range(2):
        for four in range(fours):
            wide = beside[side, four].astype(F32)
            for one in range(4):
                value = wide[:, one * rank : (one + 1) * rank]
                at = side * sections + 4 * four + one
                left[at] = jnp.concatenate([value, zero], axis=1).astype(BF16)
                right[at] = jnp.concatenate([zero, value], axis=1).astype(BF16)

    def slot(j, q):
        entry = links[j, q]
        leaf = (entry // sections) & (leaves - 1)
        return jnp.where(leaf == my_leaf ^ 1, 0, sections) + (entry & (sections - 1))

    for q in range(sections):
        if q % here == 0:
            copies[2 + q // here].wait()
        pairs = [left[slot(j, q)] + right[slot(j + 1, q)] for j in range(0, link_count, 2)]
        wide = jnp.concatenate(pairs, axis=1)
        coupled[q] = dot(wide, couple_w[q].reshape(link_count * rank, rank).astype(BF16))

    for copy in copies[4:8]:
        copy.wait()

    def store(at, many, total):
        out[pl.ds(at, many)] = total.reshape(many, rhs, points)

    near_sum(lambda j, b: codes[j, b], table, near_w, store)

    for copy in copies[8:11]:
        copy.wait()
    slab_tops = top_links.shape[0]
    half = rhs // 2
    lane = lax.broadcasted_iota(jnp.int32, (half, 2 * rank), 1) < rank
    sums = []
    for j in range(link_count):
        link = top_links[my_top, j]
        first = (link & (slab_tops - 1)) * (GROUP * slabs) + link // slab_tops
        sums.append(sum(tops_v[first + one * slabs].astype(F32) for one in range(GROUP)))
    wide = []
    for j in range(0, link_count, 2):
        upper = jnp.where(lane, sums[j], pltpu.roll(sums[j + 1], rank, 1))
        lower = jnp.where(lane, pltpu.roll(sums[j], rank, 1), sums[j + 1])
        wide.append(jnp.concatenate([upper, lower], axis=0))
    local = dot_split(jnp.concatenate(wide, axis=1), coupler[...].reshape(link_count * rank, rank))
    for q in range(sections):
        value = dot_split(local, section_w[q]) + coupled[q]
        tables[0, q], tables[1, q] = split(jnp.concatenate([value, zero], axis=1))
        tables[2, q], tables[3, q] = split(jnp.concatenate([zero, value], axis=1))

    for copy in copies[11:]:
        copy.wait()
    mask = own_mask(rhs, rank)
    none = jnp.zeros((rhs, 2 * rank), BF16)
    for four in range(count // 4):
        slots = [parent[4 * four + one] & (sections - 1) for one in range(4)]
        lines = []
        for part in range(2):
            a, b = tables.at[part], tables.at[2 + part]
            lines += [
                jnp.concatenate([a[slots[0]], none], axis=1),
                jnp.concatenate([b[slots[1]], none], axis=1),
                jnp.concatenate([none, a[slots[2]]], axis=1),
                jnp.concatenate([none, b[slots[3]]], axis=1),
            ]
        w_hi, w_lo = split(leaf_w[4 * four : 4 * four + 4].reshape(4 * rank, rank))
        both = dot(jnp.concatenate(lines, axis=0), w_hi)
        value = both[: 4 * rhs] + both[4 * rhs :] + dot(jnp.concatenate(lines[:4], axis=0), w_lo)
        double = jnp.concatenate([value, value], axis=1)
        spread[four] = jnp.where(mask, jnp.concatenate([double, double], axis=1), 0.0).astype(BF16)
    for four in range(count // 4):
        at = pl.ds(4 * four, 4)
        far = dot(spread[four], target_w[4 * four : 4 * four + 4].reshape(4 * rank, points))
        out[at] += far.reshape(4, rhs, points)


def local_call(
    parent, top_links, links, codes, inner, outer, coupling, from_low, own_src, from_high, near_blocks,
    tops, couplers, down_section, down_leaf, target,
):
    rhs = own_src.shape[1]
    count, rank, points = target.shape
    sections = coupling.shape[0]
    return pl.pallas_call(
        local_kernel,
        in_specs=[SMEM] * 4 + [HBM] * 12,
        out_specs=VMEM,
        out_shape=jax.ShapeDtypeStruct((count, rhs, points), F32),
        scratch_shapes=[
            pltpu.VMEM((3 * count + 1, rhs, points), BF16),
            pltpu.VMEM(near_blocks.shape, BF16),
            pltpu.VMEM((2, sections // 4, rhs, points), BF16),
            pltpu.VMEM(coupling.shape, F32),
            pltpu.VMEM(tops.shape, BF16),
            pltpu.VMEM(couplers.shape[1:], F32),
            pltpu.VMEM(down_section.shape, F32),
            pltpu.VMEM(down_leaf.shape, F32),
            pltpu.VMEM(target.shape, BF16),
            pltpu.VMEM((2 * sections, rhs, 2 * rank), BF16),
            pltpu.VMEM((2 * sections, rhs, 2 * rank), BF16),
            pltpu.VMEM((sections, rhs, rank), F32),
            pltpu.VMEM((4, sections, rhs, 2 * rank), BF16),
            pltpu.VMEM((count // 4, 4 * rhs, 4 * rank), BF16),
            pltpu.SemaphoreType.DMA((13,)),
        ],
        compiler_params=params(56),
        cost_estimate=cost(40),
        name="local",
    )(
        parent, top_links, links, codes, inner, outer, coupling, from_low, own_src, from_high, near_blocks,
        tops, couplers, down_section, down_leaf, target,
    )


def shifted(x, axis, step):
    count = lax.axis_size(axis)
    return lax.ppermute(x, axis, [(i, (i + step) % count) for i in range(count)])


def swapped(x, first):
    count = lax.axis_size("leaf")
    return lax.ppermute(
        x, "leaf", [(i, (i + (1 if i % 2 == first else -1)) % count) for i in range(count)]
    )


def shards(
    sources, source_basis, target_basis, up_leaf, down_leaf, up_section, down_section,
    section_coupling, top_coupling, near_blocks, leaf_parent, near_list, section_list, top_list,
):
    devices = lax.axis_size("leaf") * lax.axis_size("slab")
    near_list = near_list.T
    from_low = shifted(sources, "slab", 1)
    from_high = shifted(sources, "slab", -1)
    to_inner, to_outer, sent = moments_call(
        leaf_parent, sources, source_basis, up_leaf, up_section, near_list, devices
    )
    inner = swapped(to_inner, 0)
    outer = swapped(to_outer, 1)
    tops = lax.all_to_all(sent, ("leaf", "slab"), 0, 0, tiled=True)
    near_inner, near_outer, codes = beside_call(
        inner, outer, from_low, sources, from_high, near_list, near_blocks
    )
    near_inner = swapped(near_inner, 0)
    near_outer = swapped(near_outer, 1)
    local = local_call(
        leaf_parent, top_list, section_list.T, codes, inner, outer, section_coupling, from_low, sources,
        from_high, near_blocks, tops, top_coupling, down_section, down_leaf, target_basis,
    )
    return (local + near_inner.astype(F32) + near_outer.astype(F32)).astype(BF16)


def solution(mesh):
    in_specs = (
        P(("slab", "leaf"), None, None),
        P(("slab", "leaf"), None, None),
        P(("slab", "leaf"), None, None),
        P(("slab", "leaf"), None, None),
        P(("slab", "leaf"), None, None),
        P(("slab", "leaf"), None, None),
        P(("slab", "leaf"), None, None),
        P(("slab", "leaf"), None, None, None),
        P("slab", None, None, None),
        P(),
        P(("slab", "leaf")),
        P(("slab", "leaf"), None),
        P(("slab", "leaf"), None),
        P("slab", None),
    )
    out_specs = P(("slab", "leaf"), None, None)
    return jax.shard_map(shards, mesh=mesh, in_specs=in_specs, out_specs=out_specs, check_vma=False)
```

```python
import jax
import jax.numpy as jnp
from jax import lax
from jax.experimental import pallas as pl
from jax.experimental.pallas import tpu as pltpu
from jax.sharding import PartitionSpec as P

GROUP = 4
F32 = jnp.float32
BF16 = jnp.bfloat16
HBM = pl.BlockSpec(memory_space=pltpu.HBM)
VMEM = pl.BlockSpec(memory_space=pltpu.VMEM)
SMEM = pl.BlockSpec(memory_space=pltpu.SMEM)
LISTS = 4
PACK = 32


def params(mib=64):
    return pltpu.CompilerParams(vmem_limit_bytes=mib * 1024 * 1024)


def cost(us):
    return pl.CostEstimate(flops=int(us * 1_000_000_000), bytes_accessed=0, transcendentals=0)


def dot(a, b):
    return jnp.dot(a, b, preferred_element_type=F32)


def split(x):
    hi = x.astype(BF16)
    return hi, (x - hi.astype(F32)).astype(BF16)


def dot_split(x, w):
    rows = x.shape[0]
    hi, lo = split(x)
    w_hi, w_lo = split(w)
    both = dot(jnp.concatenate([hi, lo], axis=0), w_hi)
    return both[:rows] + both[rows:] + dot(hi, w_lo)


def own_mask(rhs, rank):
    row = lax.broadcasted_iota(jnp.int32, (4 * rhs, 4 * rank), 0) // rhs
    col = lax.broadcasted_iota(jnp.int32, (4 * rhs, 4 * rank), 1) // rank
    return row == col


def started(pairs, sems):
    copies = [pltpu.make_async_copy(ref, buf, sems.at[k]) for k, (ref, buf) in enumerate(pairs)]
    for copy in copies:
        copy.start()
    return copies


def list_place(entries, count):
    my_leaf = lax.axis_index("leaf")
    my_slab = lax.axis_index("slab")
    leaves = lax.axis_size("leaf")
    slabs = lax.axis_size("slab")
    owner = entries // count
    rel_slab = (owner // leaves - my_slab + 1) & (slabs - 1)
    rel_leaf = ((owner & (leaves - 1)) - my_leaf + 1) & (leaves - 1)
    return rel_leaf, rel_slab * count + (entries & (count - 1))


def moments_kernel(
    parent, sources, source_basis, up_leaf, up_section, near_list, to_inner, to_outer, top,
    src, basis, lift, raise_, lists, total, sems,
):
    count, rhs, points = src.shape
    rank = basis.shape[1]
    sections = total.shape[0]
    chunks = 2
    boxes = count // chunks
    pairs = []
    for c in range(chunks):
        at = pl.ds(c * boxes, boxes)
        pairs += [(ref.at[at], buf.at[at]) for ref, buf in ((sources, src), (source_basis, basis), (up_leaf, lift))]
        if c == 0:
            pairs += [(near_list, lists), (up_section, raise_)]
    copies = started(pairs, sems)
    total[...] = jnp.zeros_like(total)
    to_inner[...] = jnp.zeros_like(to_inner)
    to_outer[...] = jnp.zeros_like(to_outer)
    own = own_mask(rhs, rank)
    at_copy = 0
    for c in range(chunks):
        many = 5 if c == 0 else 3
        for copy in copies[at_copy : at_copy + many]:
            copy.wait()
        at_copy += many
        parts = [slice(c * boxes + 4 * f, c * boxes + 4 * f + 4) for f in range(boxes // 4)]
        crossed = [
            lax.dot_general(
                src[part].reshape(4 * rhs, points),
                basis[part].reshape(4 * rank, points),
                (((1,), (1,)), ((), ())),
                preferred_element_type=F32,
            )
            for part in parts
        ]
        lifted = [
            dot_split(jnp.where(own, x, 0.0), lift[part].reshape(4 * rank, rank))
            for x, part in zip(crossed, parts)
        ]
        for f, x in enumerate(lifted):
            for one in range(4):
                slot = parent[c * boxes + 4 * f + one] & (sections - 1)
                total[slot] += x[one * rhs : (one + 1) * rhs]
    fours = sections // 4
    for four in range(fours):
        wide = jnp.concatenate([total[4 * four + one] for one in range(4)], axis=1)
        for ref in (to_inner, to_outer):
            ref[four], ref[LISTS + 1 + four] = split(wide)
        term = dot_split(wide, raise_[4 * four : 4 * four + 4].reshape(4 * rank, rank))
        partial = term if four == 0 else partial + term
    half = rhs // 2
    packed = jnp.concatenate([partial[:half], partial[half:]], axis=1).astype(BF16)
    top[...] = jnp.broadcast_to(packed[None], top.shape)

    entries = lists[...]
    rel_leaf, place = list_place(entries, count)
    rows, boxes = entries.shape
    odd = lax.axis_index("leaf") & 1
    for ref, step in ((to_inner, 2 - 2 * odd), (to_outer, 2 * odd)):
        ref[fours, :rows, :boxes] = jnp.where(rel_leaf == step, place, 3 * count).astype(F32).astype(BF16)


def moments_call(parent, sources, source_basis, up_leaf, up_section, near_list, devices):
    count, rhs, points = sources.shape
    rank = source_basis.shape[1]
    sections = up_section.shape[0]
    pack = jax.ShapeDtypeStruct((PACK, rhs, points), BF16)
    return pl.pallas_call(
        moments_kernel,
        in_specs=[SMEM, HBM, HBM, HBM, HBM, HBM],
        out_specs=[VMEM, VMEM, VMEM],
        out_shape=[pack, pack, jax.ShapeDtypeStruct((devices, rhs // 2, 2 * rank), BF16)],
        scratch_shapes=[
            pltpu.VMEM(sources.shape, BF16),
            pltpu.VMEM(source_basis.shape, BF16),
            pltpu.VMEM(up_leaf.shape, F32),
            pltpu.VMEM(up_section.shape, F32),
            pltpu.VMEM(near_list.shape, jnp.int32),
            pltpu.VMEM((sections, rhs, rank), F32),
            pltpu.SemaphoreType.DMA((14,)),
        ],
        compiler_params=params(),
        cost_estimate=cost(0),
        name="moments",
    )(parent, sources, source_basis, up_leaf, up_section, near_list)


def near_sum(codes, table, near_blocks, store):
    entries = near_blocks.shape[0]
    count = 64
    chunk = 16
    for part in range(count // chunk):
        for j in range(entries):
            rows = jnp.concatenate([table[codes(j, part * chunk + b)] for b in range(chunk)], axis=0)
            term = dot(rows, near_blocks[j])
            total = term if j == 0 else total + term
        store(part * chunk, chunk, total)


def beside_kernel(
    inner, outer, from_low, own_src, from_high, near_list, near_blocks,
    to_inner, to_outer, own_codes, table, near_w, lists, entries, coded, codes, sems, code_sems,
):
    count, rhs, points = own_src.shape
    fours = LISTS
    copies = started(
        (
            (inner.at[fours], lists.at[0]), (outer.at[fours], lists.at[1]), (near_list, entries),
            (near_blocks, near_w),
            (from_low, table.at[pl.ds(0, count)]),
            (own_src, table.at[pl.ds(count, count)]),
            (from_high, table.at[pl.ds(2 * count, count)]),
        ),
        sems,
    )
    table[3 * count] = jnp.zeros((rhs, points), BF16)
    for copy in copies[:3]:
        copy.wait()
    rel_leaf, place = list_place(entries[...], count)
    own_codes[...] = jnp.where(rel_leaf == 1, place, 3 * count)
    for k in range(2):
        coded[k] = lists[k].astype(F32).astype(jnp.int32)[:, :128]
    moves = [pltpu.make_async_copy(coded.at[k], codes.at[k], code_sems.at[k]) for k in range(2)]
    for move in moves:
        move.start()
    for copy in copies[3:]:
        copy.wait()
    for move in moves:
        move.wait()
    for k, out in enumerate((to_inner, to_outer)):
        def store(at, many, total, out=out):
            out[pl.ds(at, many)] = total.astype(BF16).reshape(many, rhs, points)

        near_sum(lambda j, b, k=k: codes[k, j, b], table, near_w, store)


def beside_call(inner, outer, from_low, own_src, from_high, near_list, near_blocks):
    count, rhs, points = own_src.shape
    block = jax.ShapeDtypeStruct(own_src.shape, BF16)
    return pl.pallas_call(
        beside_kernel,
        in_specs=[HBM] * 7,
        out_specs=[VMEM] * 3,
        out_shape=[block, block, jax.ShapeDtypeStruct(near_list.shape, jnp.int32)],
        scratch_shapes=[
            pltpu.VMEM((3 * count + 1, rhs, points), BF16),
            pltpu.VMEM(near_blocks.shape, BF16),
            pltpu.VMEM((2, rhs, points), BF16),
            pltpu.VMEM(near_list.shape, jnp.int32),
            pltpu.VMEM((2, rhs, 128), jnp.int32),
            pltpu.SMEM((2, rhs, 128), jnp.int32),
            pltpu.SemaphoreType.DMA((7,)),
            pltpu.SemaphoreType.DMA((2,)),
        ],
        compiler_params=params(),
        cost_estimate=cost(0),
        name="beside",
    )(inner, outer, from_low, own_src, from_high, near_list, near_blocks)


def local_kernel(
    parent, top_links, links, codes,
    inner, outer, coupling, from_low, own_src, from_high, near_blocks, tops, couplers, down_section,
    down_leaf, target, out,
    table, near_w, beside, couple_w, tops_v, coupler, section_w, leaf_w, target_w,
    left, right, coupled, tables, spread, sems,
):
    count, rhs, points = out.shape
    rank = target.shape[1]
    sections, link_count = coupling.shape[:2]
    fours = sections // 4
    my_leaf = lax.axis_index("leaf")
    leaves = lax.axis_size("leaf")
    slabs = lax.axis_size("slab")
    my_top = my_leaf // GROUP
    parts = pl.ds(0, LISTS + 1 + fours)
    chunks = 2
    here = sections // chunks
    pairs = [
        (near_blocks, near_w),
        (from_low, table.at[pl.ds(0, count)]),
        (own_src, table.at[pl.ds(count, count)]),
        (from_high, table.at[pl.ds(2 * count, count)]),
        (inner.at[parts], beside.at[0]), (outer.at[parts], beside.at[1]),
    ]
    for c in range(chunks):
        at = pl.ds(c * here, here)
        pairs.append((coupling.at[at], couple_w.at[at]))
    pairs += [
        (tops, tops_v), (couplers.at[my_top], coupler), (down_section, section_w),
        (down_leaf, leaf_w), (target, target_w),
    ]
    copies = started(pairs, sems)

    table[3 * count] = jnp.zeros((rhs, points), BF16)

    for copy in copies[:4]:
        copy.wait()

    def store(at, many, total):
        out[pl.ds(at, many)] = total.reshape(many, rhs, points)

    near_sum(lambda j, b: codes[j, b], table, near_w, store)

    for copy in copies[4:6]:
        copy.wait()
    zero = jnp.zeros((rhs, rank), F32)
    for side in range(2):
        for part in range(2):
            for four in range(fours):
                wide = beside[side, part * (LISTS + 1) + four].astype(F32)
                for one in range(4):
                    value = wide[:, one * rank : (one + 1) * rank]
                    at = side * sections + 4 * four + one
                    left[part, at] = jnp.concatenate([value, zero], axis=1).astype(BF16)
                    right[part, at] = jnp.concatenate([zero, value], axis=1).astype(BF16)

    def slot(j, q):
        entry = links[j, q]
        leaf = (entry // sections) & (leaves - 1)
        return jnp.where(leaf == my_leaf ^ 1, 0, sections) + (entry & (sections - 1))

    for q in range(sections):
        if q % here == 0:
            copies[6 + q // here].wait()
        slots = [slot(j, q) for j in range(link_count)]
        lines = []
        for part in range(2):
            pairs = [left[part, slots[j]] + right[part, slots[j + 1]] for j in range(0, link_count, 2)]
            lines.append(jnp.concatenate(pairs, axis=1))
        weights = couple_w[q].reshape(link_count * rank, rank).astype(BF16)
        both = dot(jnp.concatenate(lines, axis=0), weights)
        coupled[q] = both[:rhs] + both[rhs:]

    for copy in copies[8:11]:
        copy.wait()
    slab_tops = top_links.shape[0]
    half = rhs // 2
    lane = lax.broadcasted_iota(jnp.int32, (half, 2 * rank), 1) < rank
    sums = []
    for j in range(link_count):
        link = top_links[my_top, j]
        first = (link & (slab_tops - 1)) * (GROUP * slabs) + link // slab_tops
        sums.append(sum(tops_v[first + one * slabs].astype(F32) for one in range(GROUP)))
    wide = []
    for j in range(0, link_count, 2):
        upper = jnp.where(lane, sums[j], pltpu.roll(sums[j + 1], rank, 1))
        lower = jnp.where(lane, pltpu.roll(sums[j], rank, 1), sums[j + 1])
        wide.append(jnp.concatenate([upper, lower], axis=0))
    local = dot_split(jnp.concatenate(wide, axis=1), coupler[...].reshape(link_count * rank, rank))
    for q in range(sections):
        value = dot_split(local, section_w[q]) + coupled[q]
        tables[0, q], tables[1, q] = split(jnp.concatenate([value, zero], axis=1))
        tables[2, q], tables[3, q] = split(jnp.concatenate([zero, value], axis=1))

    for copy in copies[11:]:
        copy.wait()
    mask = own_mask(rhs, rank)
    none = jnp.zeros((rhs, 2 * rank), BF16)
    for four in range(count // 4):
        slots = [parent[4 * four + one] & (sections - 1) for one in range(4)]
        lines = []
        for part in range(2):
            a, b = tables.at[part], tables.at[2 + part]
            lines += [
                jnp.concatenate([a[slots[0]], none], axis=1),
                jnp.concatenate([b[slots[1]], none], axis=1),
                jnp.concatenate([none, a[slots[2]]], axis=1),
                jnp.concatenate([none, b[slots[3]]], axis=1),
            ]
        w_hi, w_lo = split(leaf_w[4 * four : 4 * four + 4].reshape(4 * rank, rank))
        both = dot(jnp.concatenate(lines, axis=0), w_hi)
        value = both[: 4 * rhs] + both[4 * rhs :] + dot(jnp.concatenate(lines[:4], axis=0), w_lo)
        double = jnp.concatenate([value, value], axis=1)
        spread[four] = jnp.where(mask, jnp.concatenate([double, double], axis=1), 0.0).astype(BF16)
    for four in range(count // 4):
        at = pl.ds(4 * four, 4)
        far = dot(spread[four], target_w[4 * four : 4 * four + 4].reshape(4 * rank, points))
        out[at] += far.reshape(4, rhs, points)


def local_call(
    parent, top_links, links, codes, inner, outer, coupling, from_low, own_src, from_high, near_blocks,
    tops, couplers, down_section, down_leaf, target,
):
    rhs = own_src.shape[1]
    count, rank, points = target.shape
    sections = coupling.shape[0]
    return pl.pallas_call(
        local_kernel,
        in_specs=[SMEM] * 4 + [HBM] * 12,
        out_specs=VMEM,
        out_shape=jax.ShapeDtypeStruct((count, rhs, points), F32),
        scratch_shapes=[
            pltpu.VMEM((3 * count + 1, rhs, points), BF16),
            pltpu.VMEM(near_blocks.shape, BF16),
            pltpu.VMEM((2, LISTS + 1 + sections // 4, rhs, points), BF16),
            pltpu.VMEM(coupling.shape, F32),
            pltpu.VMEM(tops.shape, BF16),
            pltpu.VMEM(couplers.shape[1:], F32),
            pltpu.VMEM(down_section.shape, F32),
            pltpu.VMEM(down_leaf.shape, F32),
            pltpu.VMEM(target.shape, BF16),
            pltpu.VMEM((2, 2 * sections, rhs, 2 * rank), BF16),
            pltpu.VMEM((2, 2 * sections, rhs, 2 * rank), BF16),
            pltpu.VMEM((sections, rhs, rank), F32),
            pltpu.VMEM((4, sections, rhs, 2 * rank), BF16),
            pltpu.VMEM((count // 4, 4 * rhs, 4 * rank), BF16),
            pltpu.SemaphoreType.DMA((13,)),
        ],
        compiler_params=params(56),
        cost_estimate=cost(40),
        name="local",
    )(
        parent, top_links, links, codes, inner, outer, coupling, from_low, own_src, from_high, near_blocks,
        tops, couplers, down_section, down_leaf, target,
    )


def shifted(x, axis, step):
    count = lax.axis_size(axis)
    return lax.ppermute(x, axis, [(i, (i + step) % count) for i in range(count)])


def swapped(x, first):
    count = lax.axis_size("leaf")
    return lax.ppermute(
        x, "leaf", [(i, (i + (1 if i % 2 == first else -1)) % count) for i in range(count)]
    )


def shards(
    sources, source_basis, target_basis, up_leaf, down_leaf, up_section, down_section,
    section_coupling, top_coupling, near_blocks, leaf_parent, near_list, section_list, top_list,
):
    devices = lax.axis_size("leaf") * lax.axis_size("slab")
    near_list = near_list.T
    from_low = shifted(sources, "slab", 1)
    from_high = shifted(sources, "slab", -1)
    to_inner, to_outer, sent = moments_call(
        leaf_parent, sources, source_basis, up_leaf, up_section, near_list, devices
    )
    inner = swapped(to_inner, 0)
    outer = swapped(to_outer, 1)
    tops = lax.all_to_all(sent, ("leaf", "slab"), 0, 0, tiled=True)
    near_inner, near_outer, codes = beside_call(
        inner, outer, from_low, sources, from_high, near_list, near_blocks
    )
    near_inner = swapped(near_inner, 0)
    near_outer = swapped(near_outer, 1)
    local = local_call(
        leaf_parent, top_list, section_list.T, codes, inner, outer, section_coupling, from_low, sources,
        from_high, near_blocks, tops, top_coupling, down_section, down_leaf, target_basis,
    )
    return (local + near_inner.astype(F32) + near_outer.astype(F32)).astype(BF16)


def solution(mesh):
    in_specs = (
        P(("slab", "leaf"), None, None),
        P(("slab", "leaf"), None, None),
        P(("slab", "leaf"), None, None),
        P(("slab", "leaf"), None, None),
        P(("slab", "leaf"), None, None),
        P(("slab", "leaf"), None, None),
        P(("slab", "leaf"), None, None),
        P(("slab", "leaf"), None, None, None),
        P("slab", None, None, None),
        P(),
        P(("slab", "leaf")),
        P(("slab", "leaf"), None),
        P(("slab", "leaf"), None),
        P("slab", None),
    )
    out_specs = P(("slab", "leaf"), None, None)
    return jax.shard_map(shards, mesh=mesh, in_specs=in_specs, out_specs=out_specs, check_vma=False)
```

```python
import jax
import jax.numpy as jnp
from jax import lax
from jax.experimental import pallas as pl
from jax.experimental.pallas import tpu as pltpu
from jax.sharding import PartitionSpec as P

GROUP = 4
F32 = jnp.float32
BF16 = jnp.bfloat16
HBM = pl.BlockSpec(memory_space=pltpu.HBM)
VMEM = pl.BlockSpec(memory_space=pltpu.VMEM)
SMEM = pl.BlockSpec(memory_space=pltpu.SMEM)
LISTS = 4
PACK = 32


def params(mib=64):
    return pltpu.CompilerParams(vmem_limit_bytes=mib * 1024 * 1024)


def cost(us):
    return pl.CostEstimate(flops=int(us * 1_000_000_000), bytes_accessed=0, transcendentals=0)


def dot(a, b):
    return jnp.dot(a, b, preferred_element_type=F32)


def split(x):
    hi = x.astype(BF16)
    return hi, (x - hi.astype(F32)).astype(BF16)


def dot_split(x, w):
    rows = x.shape[0]
    hi, lo = split(x)
    w_hi, w_lo = split(w)
    both = dot(jnp.concatenate([hi, lo], axis=0), w_hi)
    return both[:rows] + both[rows:] + dot(hi, w_lo)


def own_mask(rhs, rank):
    row = lax.broadcasted_iota(jnp.int32, (4 * rhs, 4 * rank), 0) // rhs
    col = lax.broadcasted_iota(jnp.int32, (4 * rhs, 4 * rank), 1) // rank
    return row == col


def started(pairs, sems):
    copies = [pltpu.make_async_copy(ref, buf, sems.at[k]) for k, (ref, buf) in enumerate(pairs)]
    for copy in copies:
        copy.start()
    return copies


def list_place(entries, count):
    my_leaf = lax.axis_index("leaf")
    my_slab = lax.axis_index("slab")
    leaves = lax.axis_size("leaf")
    slabs = lax.axis_size("slab")
    owner = entries // count
    rel_slab = (owner // leaves - my_slab + 1) & (slabs - 1)
    rel_leaf = ((owner & (leaves - 1)) - my_leaf + 1) & (leaves - 1)
    return rel_leaf, rel_slab * count + (entries & (count - 1))


def moments_kernel(
    parent, sources, source_basis, up_leaf, up_section, near_list, to_inner, to_outer, top,
    src, basis, lift, raise_, lists, total, sems,
):
    count, rhs, points = src.shape
    rank = basis.shape[1]
    sections = total.shape[0]
    chunks = 2
    boxes = count // chunks
    pairs = []
    for c in range(chunks):
        at = pl.ds(c * boxes, boxes)
        pairs += [(ref.at[at], buf.at[at]) for ref, buf in ((sources, src), (source_basis, basis), (up_leaf, lift))]
        if c == 0:
            pairs += [(near_list, lists), (up_section, raise_)]
    copies = started(pairs, sems)
    total[...] = jnp.zeros_like(total)
    to_inner[...] = jnp.zeros_like(to_inner)
    to_outer[...] = jnp.zeros_like(to_outer)
    own = own_mask(rhs, rank)
    at_copy = 0
    for c in range(chunks):
        many = 5 if c == 0 else 3
        for copy in copies[at_copy : at_copy + many]:
            copy.wait()
        at_copy += many
        parts = [slice(c * boxes + 4 * f, c * boxes + 4 * f + 4) for f in range(boxes // 4)]
        crossed = [
            lax.dot_general(
                src[part].reshape(4 * rhs, points),
                basis[part].reshape(4 * rank, points),
                (((1,), (1,)), ((), ())),
                preferred_element_type=F32,
            )
            for part in parts
        ]
        lifted = [
            dot_split(jnp.where(own, x, 0.0), lift[part].reshape(4 * rank, rank))
            for x, part in zip(crossed, parts)
        ]
        for f, x in enumerate(lifted):
            for one in range(4):
                slot = parent[c * boxes + 4 * f + one] & (sections - 1)
                total[slot] += x[one * rhs : (one + 1) * rhs]
    fours = sections // 4
    for four in range(fours):
        wide = jnp.concatenate([total[4 * four + one] for one in range(4)], axis=1)
        for ref in (to_inner, to_outer):
            ref[four], ref[LISTS + 1 + four] = split(wide)
        term = dot_split(wide, raise_[4 * four : 4 * four + 4].reshape(4 * rank, rank))
        partial = term if four == 0 else partial + term
    half = rhs // 2
    packed = jnp.concatenate([partial[:half], partial[half:]], axis=1).astype(BF16)
    top[...] = jnp.broadcast_to(packed[None], top.shape)

    entries = lists[...]
    rel_leaf, place = list_place(entries, count)
    rows, boxes = entries.shape
    odd = lax.axis_index("leaf") & 1
    for ref, step in ((to_inner, 2 - 2 * odd), (to_outer, 2 * odd)):
        ref[fours, :rows, :boxes] = jnp.where(rel_leaf == step, place, 3 * count).astype(F32).astype(BF16)


def moments_call(parent, sources, source_basis, up_leaf, up_section, near_list, devices):
    count, rhs, points = sources.shape
    rank = source_basis.shape[1]
    sections = up_section.shape[0]
    pack = jax.ShapeDtypeStruct((PACK, rhs, points), BF16)
    return pl.pallas_call(
        moments_kernel,
        in_specs=[SMEM, HBM, HBM, HBM, HBM, HBM],
        out_specs=[VMEM, VMEM, VMEM],
        out_shape=[pack, pack, jax.ShapeDtypeStruct((devices, rhs // 2, 2 * rank), BF16)],
        scratch_shapes=[
            pltpu.VMEM(sources.shape, BF16),
            pltpu.VMEM(source_basis.shape, BF16),
            pltpu.VMEM(up_leaf.shape, F32),
            pltpu.VMEM(up_section.shape, F32),
            pltpu.VMEM(near_list.shape, jnp.int32),
            pltpu.VMEM((sections, rhs, rank), F32),
            pltpu.SemaphoreType.DMA((14,)),
        ],
        compiler_params=params(),
        cost_estimate=cost(0),
        name="moments",
    )(parent, sources, source_basis, up_leaf, up_section, near_list)


def near_sum(codes, table, near_blocks, store):
    entries = near_blocks.shape[0]
    count = 64
    chunk = 16
    for part in range(count // chunk):
        for j in range(entries):
            rows = jnp.concatenate([table[codes(j, part * chunk + b)] for b in range(chunk)], axis=0)
            term = dot(rows, near_blocks[j])
            total = term if j == 0 else total + term
        store(part * chunk, chunk, total)


def beside_kernel(
    inner, outer, from_low, own_src, from_high, near_list, near_blocks,
    to_inner, to_outer, own_codes, table, near_w, lists, entries, coded, codes, sems, code_sems,
):
    count, rhs, points = own_src.shape
    fours = LISTS
    copies = started(
        (
            (inner.at[fours], lists.at[0]), (outer.at[fours], lists.at[1]), (near_list, entries),
            (near_blocks, near_w),
            (from_low, table.at[pl.ds(0, count)]),
            (own_src, table.at[pl.ds(count, count)]),
            (from_high, table.at[pl.ds(2 * count, count)]),
        ),
        sems,
    )
    table[3 * count] = jnp.zeros((rhs, points), BF16)
    for copy in copies[:3]:
        copy.wait()
    rel_leaf, place = list_place(entries[...], count)
    own_codes[...] = jnp.where(rel_leaf == 1, place, 3 * count)
    for k in range(2):
        coded[k] = lists[k].astype(F32).astype(jnp.int32)[:, :128]
    moves = [pltpu.make_async_copy(coded.at[k], codes.at[k], code_sems.at[k]) for k in range(2)]
    for move in moves:
        move.start()
    for copy in copies[3:]:
        copy.wait()
    for move in moves:
        move.wait()
    for k, out in enumerate((to_inner, to_outer)):
        def store(at, many, total, out=out):
            out[pl.ds(at, many)] = total.astype(BF16).reshape(many, rhs, points)

        near_sum(lambda j, b, k=k: codes[k, j, b], table, near_w, store)


def beside_call(inner, outer, from_low, own_src, from_high, near_list, near_blocks):
    count, rhs, points = own_src.shape
    block = jax.ShapeDtypeStruct(own_src.shape, BF16)
    return pl.pallas_call(
        beside_kernel,
        in_specs=[HBM] * 7,
        out_specs=[VMEM] * 3,
        out_shape=[block, block, jax.ShapeDtypeStruct(near_list.shape, jnp.int32)],
        scratch_shapes=[
            pltpu.VMEM((3 * count + 1, rhs, points), BF16),
            pltpu.VMEM(near_blocks.shape, BF16),
            pltpu.VMEM((2, rhs, points), BF16),
            pltpu.VMEM(near_list.shape, jnp.int32),
            pltpu.VMEM((2, rhs, 128), jnp.int32),
            pltpu.SMEM((2, rhs, 128), jnp.int32),
            pltpu.SemaphoreType.DMA((7,)),
            pltpu.SemaphoreType.DMA((2,)),
        ],
        compiler_params=params(),
        cost_estimate=cost(0),
        name="beside",
    )(inner, outer, from_low, own_src, from_high, near_list, near_blocks)


def local_kernel(
    parent, top_links, links, codes,
    inner, outer, coupling, from_low, own_src, from_high, near_blocks, tops, couplers, down_section,
    down_leaf, target, out,
    held, table, near_w, beside, couple_w, tops_v, coupler, section_w, leaf_w, target_w,
    left, right, coupled, tables, spread, sems,
):
    count, rhs, points = out.shape
    rank = target.shape[1]
    sections, link_count = coupling.shape[:2]
    fours = sections // 4
    my_leaf = lax.axis_index("leaf")
    leaves = lax.axis_size("leaf")
    slabs = lax.axis_size("slab")
    my_top = my_leaf // GROUP
    parts = pl.ds(0, LISTS + 1 + fours)
    chunks = 1
    here = sections // chunks
    pairs = [
        (near_blocks, near_w),
        (from_low, table.at[pl.ds(0, count)]),
        (own_src, table.at[pl.ds(count, count)]),
        (from_high, table.at[pl.ds(2 * count, count)]),
        (inner.at[parts], beside.at[0]), (outer.at[parts], beside.at[1]),
    ]
    for c in range(chunks):
        at = pl.ds(c * here, here)
        pairs.append((coupling.at[at], couple_w.at[at]))
    pairs += [
        (tops, tops_v), (couplers.at[my_top], coupler), (down_section, section_w),
        (down_leaf, leaf_w), (target, target_w),
    ]
    copies = started(pairs, sems)

    table[3 * count] = jnp.zeros((rhs, points), BF16)

    for copy in copies[:4]:
        copy.wait()

    def store(at, many, total):
        held[pl.ds(at, many)] = total.reshape(many, rhs, points)

    near_sum(lambda j, b: codes[j, b], table, near_w, store)

    for copy in copies[4:6]:
        copy.wait()
    zero = jnp.zeros((rhs, rank), F32)
    for side in range(2):
        for part in range(2):
            for four in range(fours):
                wide = beside[side, part * (LISTS + 1) + four].astype(F32)
                for one in range(4):
                    value = wide[:, one * rank : (one + 1) * rank]
                    at = side * sections + 4 * four + one
                    left[part, at] = jnp.concatenate([value, zero], axis=1).astype(BF16)
                    right[part, at] = jnp.concatenate([zero, value], axis=1).astype(BF16)

    def slot(j, q):
        entry = links[j, q]
        leaf = (entry // sections) & (leaves - 1)
        return jnp.where(leaf == my_leaf ^ 1, 0, sections) + (entry & (sections - 1))

    for q in range(sections):
        if q % here == 0:
            copies[6 + q // here].wait()
        slots = [slot(j, q) for j in range(link_count)]
        lines = []
        for part in range(2):
            pairs = [left[part, slots[j]] + right[part, slots[j + 1]] for j in range(0, link_count, 2)]
            lines.append(jnp.concatenate(pairs, axis=1))
        weights = couple_w[q].reshape(link_count * rank, rank).astype(BF16)
        both = dot(jnp.concatenate(lines, axis=0), weights)
        coupled[q] = both[:rhs] + both[rhs:]

    for copy in copies[7:10]:
        copy.wait()
    slab_tops = top_links.shape[0]
    half = rhs // 2
    lane = lax.broadcasted_iota(jnp.int32, (half, 2 * rank), 1) < rank
    sums = []
    for j in range(link_count):
        link = top_links[my_top, j]
        first = (link & (slab_tops - 1)) * (GROUP * slabs) + link // slab_tops
        sums.append(sum(tops_v[first + one * slabs].astype(F32) for one in range(GROUP)))
    wide = []
    for j in range(0, link_count, 2):
        upper = jnp.where(lane, sums[j], pltpu.roll(sums[j + 1], rank, 1))
        lower = jnp.where(lane, pltpu.roll(sums[j], rank, 1), sums[j + 1])
        wide.append(jnp.concatenate([upper, lower], axis=0))
    local = dot_split(jnp.concatenate(wide, axis=1), coupler[...].reshape(link_count * rank, rank))
    for q in range(sections):
        value = dot_split(local, section_w[q]) + coupled[q]
        tables[0, q], tables[1, q] = split(jnp.concatenate([value, zero], axis=1))
        tables[2, q], tables[3, q] = split(jnp.concatenate([zero, value], axis=1))

    for copy in copies[10:]:
        copy.wait()
    mask = own_mask(rhs, rank)
    none = jnp.zeros((rhs, 2 * rank), BF16)
    for four in range(count // 4):
        slots = [parent[4 * four + one] & (sections - 1) for one in range(4)]
        lines = []
        for part in range(2):
            a, b = tables.at[part], tables.at[2 + part]
            lines += [
                jnp.concatenate([a[slots[0]], none], axis=1),
                jnp.concatenate([b[slots[1]], none], axis=1),
                jnp.concatenate([none, a[slots[2]]], axis=1),
                jnp.concatenate([none, b[slots[3]]], axis=1),
            ]
        w_hi, w_lo = split(leaf_w[4 * four : 4 * four + 4].reshape(4 * rank, rank))
        both = dot(jnp.concatenate(lines, axis=0), w_hi)
        value = both[: 4 * rhs] + both[4 * rhs :] + dot(jnp.concatenate(lines[:4], axis=0), w_lo)
        double = jnp.concatenate([value, value], axis=1)
        spread[four] = jnp.where(mask, jnp.concatenate([double, double], axis=1), 0.0).astype(BF16)
    for four in range(count // 4):
        at = pl.ds(4 * four, 4)
        far = dot(spread[four], target_w[4 * four : 4 * four + 4].reshape(4 * rank, points))
        out[at] = (held[at] + far.reshape(4, rhs, points)).astype(BF16)


def local_call(
    parent, top_links, links, codes, inner, outer, coupling, from_low, own_src, from_high, near_blocks,
    tops, couplers, down_section, down_leaf, target,
):
    rhs = own_src.shape[1]
    count, rank, points = target.shape
    sections = coupling.shape[0]
    return pl.pallas_call(
        local_kernel,
        in_specs=[SMEM] * 4 + [HBM] * 12,
        out_specs=VMEM,
        out_shape=jax.ShapeDtypeStruct((count, rhs, points), BF16),
        scratch_shapes=[
            pltpu.VMEM((count, rhs, points), F32),
            pltpu.VMEM((3 * count + 1, rhs, points), BF16),
            pltpu.VMEM(near_blocks.shape, BF16),
            pltpu.VMEM((2, LISTS + 1 + sections // 4, rhs, points), BF16),
            pltpu.VMEM(coupling.shape, F32),
            pltpu.VMEM(tops.shape, BF16),
            pltpu.VMEM(couplers.shape[1:], F32),
            pltpu.VMEM(down_section.shape, F32),
            pltpu.VMEM(down_leaf.shape, F32),
            pltpu.VMEM(target.shape, BF16),
            pltpu.VMEM((2, 2 * sections, rhs, 2 * rank), BF16),
            pltpu.VMEM((2, 2 * sections, rhs, 2 * rank), BF16),
            pltpu.VMEM((sections, rhs, rank), F32),
            pltpu.VMEM((4, sections, rhs, 2 * rank), BF16),
            pltpu.VMEM((count // 4, 4 * rhs, 4 * rank), BF16),
            pltpu.SemaphoreType.DMA((13,)),
        ],
        compiler_params=params(56),
        cost_estimate=cost(40),
        name="local",
    )(
        parent, top_links, links, codes, inner, outer, coupling, from_low, own_src, from_high, near_blocks,
        tops, couplers, down_section, down_leaf, target,
    )


def shifted(x, axis, step):
    count = lax.axis_size(axis)
    return lax.ppermute(x, axis, [(i, (i + step) % count) for i in range(count)])


def swapped(x, first):
    count = lax.axis_size("leaf")
    return lax.ppermute(
        x, "leaf", [(i, (i + (1 if i % 2 == first else -1)) % count) for i in range(count)]
    )


def shards(
    sources, source_basis, target_basis, up_leaf, down_leaf, up_section, down_section,
    section_coupling, top_coupling, near_blocks, leaf_parent, near_list, section_list, top_list,
):
    devices = lax.axis_size("leaf") * lax.axis_size("slab")
    near_list = near_list.T
    from_low = shifted(sources, "slab", 1)
    from_high = shifted(sources, "slab", -1)
    to_inner, to_outer, sent = moments_call(
        leaf_parent, sources, source_basis, up_leaf, up_section, near_list, devices
    )
    inner = swapped(to_inner, 0)
    outer = swapped(to_outer, 1)
    tops = lax.all_to_all(sent, ("leaf", "slab"), 0, 0, tiled=True)
    near_inner, near_outer, codes = beside_call(
        inner, outer, from_low, sources, from_high, near_list, near_blocks
    )
    near_inner = swapped(near_inner, 0)
    near_outer = swapped(near_outer, 1)
    local = local_call(
        leaf_parent, top_list, section_list.T, codes, inner, outer, section_coupling, from_low, sources,
        from_high, near_blocks, tops, top_coupling, down_section, down_leaf, target_basis,
    )
    return (local.astype(F32) + near_inner.astype(F32) + near_outer.astype(F32)).astype(BF16)


def solution(mesh):
    in_specs = (
        P(("slab", "leaf"), None, None),
        P(("slab", "leaf"), None, None),
        P(("slab", "leaf"), None, None),
        P(("slab", "leaf"), None, None),
        P(("slab", "leaf"), None, None),
        P(("slab", "leaf"), None, None),
        P(("slab", "leaf"), None, None),
        P(("slab", "leaf"), None, None, None),
        P("slab", None, None, None),
        P(),
        P(("slab", "leaf")),
        P(("slab", "leaf"), None),
        P(("slab", "leaf"), None),
        P("slab", None),
    )
    out_specs = P(("slab", "leaf"), None, None)
    return jax.shard_map(shards, mesh=mesh, in_specs=in_specs, out_specs=out_specs, check_vma=False)
```

```python
import jax
import jax.numpy as jnp
from jax import lax
from jax.experimental import pallas as pl
from jax.experimental.pallas import tpu as pltpu
from jax.sharding import PartitionSpec as P

GROUP = 4
F32 = jnp.float32
BF16 = jnp.bfloat16
HBM = pl.BlockSpec(memory_space=pltpu.HBM)
VMEM = pl.BlockSpec(memory_space=pltpu.VMEM)
SMEM = pl.BlockSpec(memory_space=pltpu.SMEM)
LISTS = 4
PACK = 32


def params(mib=64):
    return pltpu.CompilerParams(vmem_limit_bytes=mib * 1024 * 1024)


def cost(us):
    return pl.CostEstimate(flops=int(us * 1_000_000_000), bytes_accessed=0, transcendentals=0)


def dot(a, b):
    return jnp.dot(a, b, preferred_element_type=F32)


def split(x):
    hi = x.astype(BF16)
    return hi, (x - hi.astype(F32)).astype(BF16)


def dot_split(x, w):
    rows = x.shape[0]
    hi, lo = split(x)
    w_hi, w_lo = split(w)
    both = dot(jnp.concatenate([hi, lo], axis=0), w_hi)
    return both[:rows] + both[rows:] + dot(hi, w_lo)


def own_mask(rhs, rank):
    row = lax.broadcasted_iota(jnp.int32, (4 * rhs, 4 * rank), 0) // rhs
    col = lax.broadcasted_iota(jnp.int32, (4 * rhs, 4 * rank), 1) // rank
    return row == col


def started(pairs, sems):
    copies = [pltpu.make_async_copy(ref, buf, sems.at[k]) for k, (ref, buf) in enumerate(pairs)]
    for copy in copies:
        copy.start()
    return copies


def list_place(entries, count):
    my_leaf = lax.axis_index("leaf")
    my_slab = lax.axis_index("slab")
    leaves = lax.axis_size("leaf")
    slabs = lax.axis_size("slab")
    owner = entries // count
    rel_slab = (owner // leaves - my_slab + 1) & (slabs - 1)
    rel_leaf = ((owner & (leaves - 1)) - my_leaf + 1) & (leaves - 1)
    return rel_leaf, rel_slab * count + (entries & (count - 1))


def moments_kernel(
    parent, sources, source_basis, up_leaf, up_section, near_list, to_inner, to_outer, top,
    src, basis, lift, raise_, lists, total, sems,
):
    count, rhs, points = src.shape
    rank = basis.shape[1]
    sections = total.shape[0]
    chunks = 2
    boxes = count // chunks
    pairs = []
    for c in range(chunks):
        at = pl.ds(c * boxes, boxes)
        pairs += [(ref.at[at], buf.at[at]) for ref, buf in ((sources, src), (source_basis, basis), (up_leaf, lift))]
        if c == 0:
            pairs.append((near_list, lists))
    pairs.append((up_section, raise_))
    copies = started(pairs, sems)
    total[...] = jnp.zeros_like(total)
    to_inner[...] = jnp.zeros_like(to_inner)
    to_outer[...] = jnp.zeros_like(to_outer)
    own = own_mask(rhs, rank)
    at_copy = 0
    for c in range(chunks):
        many = 4 if c == 0 else 3
        for copy in copies[at_copy : at_copy + many]:
            copy.wait()
        at_copy += many
        parts = [slice(c * boxes + 4 * f, c * boxes + 4 * f + 4) for f in range(boxes // 4)]
        crossed = [
            lax.dot_general(
                src[part].reshape(4 * rhs, points),
                basis[part].reshape(4 * rank, points),
                (((1,), (1,)), ((), ())),
                preferred_element_type=F32,
            )
            for part in parts
        ]
        lifted = [
            dot_split(jnp.where(own, x, 0.0), lift[part].reshape(4 * rank, rank))
            for x, part in zip(crossed, parts)
        ]
        for f, x in enumerate(lifted):
            for one in range(4):
                slot = parent[c * boxes + 4 * f + one] & (sections - 1)
                total[slot] += x[one * rhs : (one + 1) * rhs]
    copies[-1].wait()
    fours = sections // 4
    for four in range(fours):
        wide = jnp.concatenate([total[4 * four + one] for one in range(4)], axis=1)
        for ref in (to_inner, to_outer):
            ref[four], ref[LISTS + 1 + four] = split(wide)
        term = dot_split(wide, raise_[4 * four : 4 * four + 4].reshape(4 * rank, rank))
        partial = term if four == 0 else partial + term
    half = rhs // 2
    packed = jnp.concatenate([partial[:half], partial[half:]], axis=1).astype(BF16)
    top[...] = jnp.broadcast_to(packed[None], top.shape)

    entries = lists[...]
    rel_leaf, place = list_place(entries, count)
    rows, boxes = entries.shape
    odd = lax.axis_index("leaf") & 1
    for ref, step in ((to_inner, 2 - 2 * odd), (to_outer, 2 * odd)):
        ref[fours, :rows, :boxes] = jnp.where(rel_leaf == step, place, 3 * count).astype(F32).astype(BF16)


def moments_call(parent, sources, source_basis, up_leaf, up_section, near_list, devices):
    count, rhs, points = sources.shape
    rank = source_basis.shape[1]
    sections = up_section.shape[0]
    pack = jax.ShapeDtypeStruct((PACK, rhs, points), BF16)
    return pl.pallas_call(
        moments_kernel,
        in_specs=[SMEM, HBM, HBM, HBM, HBM, HBM],
        out_specs=[VMEM, VMEM, VMEM],
        out_shape=[pack, pack, jax.ShapeDtypeStruct((devices, rhs // 2, 2 * rank), BF16)],
        scratch_shapes=[
            pltpu.VMEM(sources.shape, BF16),
            pltpu.VMEM(source_basis.shape, BF16),
            pltpu.VMEM(up_leaf.shape, F32),
            pltpu.VMEM(up_section.shape, F32),
            pltpu.VMEM(near_list.shape, jnp.int32),
            pltpu.VMEM((sections, rhs, rank), F32),
            pltpu.SemaphoreType.DMA((14,)),
        ],
        compiler_params=params(),
        cost_estimate=cost(0),
        name="moments",
    )(parent, sources, source_basis, up_leaf, up_section, near_list)


def near_sum(codes, table, near_blocks, store):
    entries = near_blocks.shape[0]
    count = 64
    chunk = 16
    for part in range(count // chunk):
        for j in range(entries):
            rows = jnp.concatenate([table[codes(j, part * chunk + b)] for b in range(chunk)], axis=0)
            term = dot(rows, near_blocks[j])
            total = term if j == 0 else total + term
        store(part * chunk, chunk, total)


def beside_kernel(
    inner, outer, from_low, own_src, from_high, near_list, near_blocks,
    to_inner, to_outer, own_codes, table, near_w, lists, entries, coded, codes, sems, code_sems,
):
    count, rhs, points = own_src.shape
    fours = LISTS
    copies = started(
        (
            (inner.at[fours], lists.at[0]), (outer.at[fours], lists.at[1]), (near_list, entries),
            (near_blocks, near_w),
            (from_low, table.at[pl.ds(0, count)]),
            (own_src, table.at[pl.ds(count, count)]),
            (from_high, table.at[pl.ds(2 * count, count)]),
        ),
        sems,
    )
    table[3 * count] = jnp.zeros((rhs, points), BF16)
    for copy in copies[:3]:
        copy.wait()
    rel_leaf, place = list_place(entries[...], count)
    own_codes[...] = jnp.where(rel_leaf == 1, place, 3 * count)
    for k in range(2):
        coded[k] = lists[k].astype(F32).astype(jnp.int32)[:, :128]
    moves = [pltpu.make_async_copy(coded.at[k], codes.at[k], code_sems.at[k]) for k in range(2)]
    for move in moves:
        move.start()
    for copy in copies[3:]:
        copy.wait()
    for move in moves:
        move.wait()
    for k, out in enumerate((to_inner, to_outer)):
        def store(at, many, total, out=out):
            out[pl.ds(at, many)] = total.astype(BF16).reshape(many, rhs, points)

        near_sum(lambda j, b, k=k: codes[k, j, b], table, near_w, store)


def beside_call(inner, outer, from_low, own_src, from_high, near_list, near_blocks):
    count, rhs, points = own_src.shape
    block = jax.ShapeDtypeStruct(own_src.shape, BF16)
    return pl.pallas_call(
        beside_kernel,
        in_specs=[HBM] * 7,
        out_specs=[VMEM] * 3,
        out_shape=[block, block, jax.ShapeDtypeStruct(near_list.shape, jnp.int32)],
        scratch_shapes=[
            pltpu.VMEM((3 * count + 1, rhs, points), BF16),
            pltpu.VMEM(near_blocks.shape, BF16),
            pltpu.VMEM((2, rhs, points), BF16),
            pltpu.VMEM(near_list.shape, jnp.int32),
            pltpu.VMEM((2, rhs, 128), jnp.int32),
            pltpu.SMEM((2, rhs, 128), jnp.int32),
            pltpu.SemaphoreType.DMA((7,)),
            pltpu.SemaphoreType.DMA((2,)),
        ],
        compiler_params=params(),
        cost_estimate=cost(0),
        name="beside",
    )(inner, outer, from_low, own_src, from_high, near_list, near_blocks)


def local_kernel(
    parent, top_links, links, codes,
    inner, outer, coupling, from_low, own_src, from_high, near_blocks, tops, couplers, down_section,
    down_leaf, target, out,
    held, table, near_w, beside, couple_w, tops_v, coupler, section_w, leaf_w, target_w,
    left, right, coupled, tables, spread, sems,
):
    count, rhs, points = out.shape
    rank = target.shape[1]
    sections, link_count = coupling.shape[:2]
    fours = sections // 4
    my_leaf = lax.axis_index("leaf")
    leaves = lax.axis_size("leaf")
    slabs = lax.axis_size("slab")
    my_top = my_leaf // GROUP
    parts = pl.ds(0, LISTS + 1 + fours)
    chunks = 1
    here = sections // chunks
    pairs = [
        (near_blocks, near_w),
        (from_low, table.at[pl.ds(0, count)]),
        (own_src, table.at[pl.ds(count, count)]),
        (from_high, table.at[pl.ds(2 * count, count)]),
        (inner.at[parts], beside.at[0]), (outer.at[parts], beside.at[1]),
    ]
    for c in range(chunks):
        at = pl.ds(c * here, here)
        pairs.append((coupling.at[at], couple_w.at[at]))
    pairs += [
        (tops, tops_v), (couplers.at[my_top], coupler), (down_section, section_w),
        (down_leaf, leaf_w), (target, target_w),
    ]
    copies = started(pairs, sems)

    table[3 * count] = jnp.zeros((rhs, points), BF16)

    for copy in copies[:4]:
        copy.wait()

    def store(at, many, total):
        held[pl.ds(at, many)] = total.reshape(many, rhs, points)

    near_sum(lambda j, b: codes[j, b], table, near_w, store)

    for copy in copies[4:6]:
        copy.wait()
    zero = jnp.zeros((rhs, rank), F32)
    for side in range(2):
        for part in range(2):
            for four in range(fours):
                wide = beside[side, part * (LISTS + 1) + four].astype(F32)
                for one in range(4):
                    value = wide[:, one * rank : (one + 1) * rank]
                    at = side * sections + 4 * four + one
                    left[part, at] = jnp.concatenate([value, zero], axis=1).astype(BF16)
                    right[part, at] = jnp.concatenate([zero, value], axis=1).astype(BF16)

    def slot(j, q):
        entry = links[j, q]
        leaf = (entry // sections) & (leaves - 1)
        return jnp.where(leaf == my_leaf ^ 1, 0, sections) + (entry & (sections - 1))

    for q in range(sections):
        if q % here == 0:
            copies[6 + q // here].wait()
        slots = [slot(j, q) for j in range(link_count)]
        lines = []
        for part in range(2):
            pairs = [left[part, slots[j]] + right[part, slots[j + 1]] for j in range(0, link_count, 2)]
            lines.append(jnp.concatenate(pairs, axis=1))
        weights = couple_w[q].reshape(link_count * rank, rank).astype(BF16)
        both = dot(jnp.concatenate(lines, axis=0), weights)
        coupled[q] = both[:rhs] + both[rhs:]

    for copy in copies[7:10]:
        copy.wait()
    slab_tops = top_links.shape[0]
    half = rhs // 2
    lane = lax.broadcasted_iota(jnp.int32, (half, 2 * rank), 1) < rank
    sums = []
    for j in range(link_count):
        link = top_links[my_top, j]
        first = (link & (slab_tops - 1)) * (GROUP * slabs) + link // slab_tops
        sums.append(sum(tops_v[first + one * slabs].astype(F32) for one in range(GROUP)))
    wide = []
    for j in range(0, link_count, 2):
        upper = jnp.where(lane, sums[j], pltpu.roll(sums[j + 1], rank, 1))
        lower = jnp.where(lane, pltpu.roll(sums[j], rank, 1), sums[j + 1])
        wide.append(jnp.concatenate([upper, lower], axis=0))
    local = dot_split(jnp.concatenate(wide, axis=1), coupler[...].reshape(link_count * rank, rank))
    for q in range(sections):
        value = dot_split(local, section_w[q]) + coupled[q]
        tables[0, q], tables[1, q] = split(jnp.concatenate([value, zero], axis=1))
        tables[2, q], tables[3, q] = split(jnp.concatenate([zero, value], axis=1))

    for copy in copies[10:]:
        copy.wait()
    mask = own_mask(rhs, rank)
    none = jnp.zeros((rhs, 2 * rank), BF16)
    for four in range(count // 4):
        slots = [parent[4 * four + one] & (sections - 1) for one in range(4)]
        lines = []
        for part in range(2):
            a, b = tables.at[part], tables.at[2 + part]
            lines += [
                jnp.concatenate([a[slots[0]], none], axis=1),
                jnp.concatenate([b[slots[1]], none], axis=1),
                jnp.concatenate([none, a[slots[2]]], axis=1),
                jnp.concatenate([none, b[slots[3]]], axis=1),
            ]
        w_hi, w_lo = split(leaf_w[4 * four : 4 * four + 4].reshape(4 * rank, rank))
        both = dot(jnp.concatenate(lines, axis=0), w_hi)
        value = both[: 4 * rhs] + both[4 * rhs :] + dot(jnp.concatenate(lines[:4], axis=0), w_lo)
        double = jnp.concatenate([value, value], axis=1)
        spread[four] = jnp.where(mask, jnp.concatenate([double, double], axis=1), 0.0).astype(BF16)
    for four in range(count // 4):
        at = pl.ds(4 * four, 4)
        far = dot(spread[four], target_w[4 * four : 4 * four + 4].reshape(4 * rank, points))
        out[at] = (held[at] + far.reshape(4, rhs, points)).astype(BF16)


def local_call(
    parent, top_links, links, codes, inner, outer, coupling, from_low, own_src, from_high, near_blocks,
    tops, couplers, down_section, down_leaf, target,
):
    rhs = own_src.shape[1]
    count, rank, points = target.shape
    sections = coupling.shape[0]
    return pl.pallas_call(
        local_kernel,
        in_specs=[SMEM] * 4 + [HBM] * 12,
        out_specs=VMEM,
        out_shape=jax.ShapeDtypeStruct((count, rhs, points), BF16),
        scratch_shapes=[
            pltpu.VMEM((count, rhs, points), F32),
            pltpu.VMEM((3 * count + 1, rhs, points), BF16),
            pltpu.VMEM(near_blocks.shape, BF16),
            pltpu.VMEM((2, LISTS + 1 + sections // 4, rhs, points), BF16),
            pltpu.VMEM(coupling.shape, F32),
            pltpu.VMEM(tops.shape, BF16),
            pltpu.VMEM(couplers.shape[1:], F32),
            pltpu.VMEM(down_section.shape, F32),
            pltpu.VMEM(down_leaf.shape, F32),
            pltpu.VMEM(target.shape, BF16),
            pltpu.VMEM((2, 2 * sections, rhs, 2 * rank), BF16),
            pltpu.VMEM((2, 2 * sections, rhs, 2 * rank), BF16),
            pltpu.VMEM((sections, rhs, rank), F32),
            pltpu.VMEM((4, sections, rhs, 2 * rank), BF16),
            pltpu.VMEM((count // 4, 4 * rhs, 4 * rank), BF16),
            pltpu.SemaphoreType.DMA((13,)),
        ],
        compiler_params=params(56),
        cost_estimate=cost(40),
        name="local",
    )(
        parent, top_links, links, codes, inner, outer, coupling, from_low, own_src, from_high, near_blocks,
        tops, couplers, down_section, down_leaf, target,
    )


def shifted(x, axis, step):
    count = lax.axis_size(axis)
    return lax.ppermute(x, axis, [(i, (i + step) % count) for i in range(count)])


def swapped(x, first):
    count = lax.axis_size("leaf")
    return lax.ppermute(
        x, "leaf", [(i, (i + (1 if i % 2 == first else -1)) % count) for i in range(count)]
    )


def shards(
    sources, source_basis, target_basis, up_leaf, down_leaf, up_section, down_section,
    section_coupling, top_coupling, near_blocks, leaf_parent, near_list, section_list, top_list,
):
    devices = lax.axis_size("leaf") * lax.axis_size("slab")
    near_list = near_list.T
    from_low = shifted(sources, "slab", 1)
    from_high = shifted(sources, "slab", -1)
    to_inner, to_outer, sent = moments_call(
        leaf_parent, sources, source_basis, up_leaf, up_section, near_list, devices
    )
    inner = swapped(to_inner, 0)
    outer = swapped(to_outer, 1)
    tops = lax.all_to_all(sent, ("leaf", "slab"), 0, 0, tiled=True)
    near_inner, near_outer, codes = beside_call(
        inner, outer, from_low, sources, from_high, near_list, near_blocks
    )
    near_inner = swapped(near_inner, 0)
    near_outer = swapped(near_outer, 1)
    local = local_call(
        leaf_parent, top_list, section_list.T, codes, inner, outer, section_coupling, from_low, sources,
        from_high, near_blocks, tops, top_coupling, down_section, down_leaf, target_basis,
    )
    return (local.astype(F32) + near_inner.astype(F32) + near_outer.astype(F32)).astype(BF16)


def solution(mesh):
    in_specs = (
        P(("slab", "leaf"), None, None),
        P(("slab", "leaf"), None, None),
        P(("slab", "leaf"), None, None),
        P(("slab", "leaf"), None, None),
        P(("slab", "leaf"), None, None),
        P(("slab", "leaf"), None, None),
        P(("slab", "leaf"), None, None),
        P(("slab", "leaf"), None, None, None),
        P("slab", None, None, None),
        P(),
        P(("slab", "leaf")),
        P(("slab", "leaf"), None),
        P(("slab", "leaf"), None),
        P("slab", None),
    )
    out_specs = P(("slab", "leaf"), None, None)
    return jax.shard_map(shards, mesh=mesh, in_specs=in_specs, out_specs=out_specs, check_vma=False)
```
